256 devices in a mesh: dp: 16 (over y, z_lo, core), cuts: 16 (over x, z_hi).
Axes of the slice: x: 4, y: 4, z: 8 (z_hi: 4, z_lo: 2; z = z_hi * 2 + z_lo), core: 2. Of those that a mesh axis runs over, the one named last changes fastest.
Arguments:
- features: bfloat16 [16, 16, 1024, 768], P('dp', None, None, 'cuts'), may hold values from -6 to 6
- lists_one: int32 [16, 16, 192, 5], P('dp'), may hold values from 0 to 1023
- lists_two: int32 [16, 16, 160, 5], P('dp', 'cuts'), may hold values from 0 to 191
- lists_three: int32 [16, 16, 128, 3], P('dp', 'cuts'), may hold values from 0 to 159
- labels: int32 [16, 16, 128], P('dp', 'cuts'), may hold values from 0 to 152
- initial_node_weight: bfloat16 [768, 1024], P('cuts'), may hold values from -0.21875 to 0.21875
- initial_neighbour_weight: bfloat16 [768, 1024], P('cuts'), may hold values from -0.21875 to 0.21875
- second_self: bfloat16 [1024, 1024], replicated, may hold values from -0.1875 to 0.1875
- second_neigh: bfloat16 [1024, 1024], replicated, may hold values from -0.1875 to 0.1875
- final_node_weight: bfloat16 [1024, 153], replicated, may hold values from -0.1875 to 0.1875
- third_neigh: bfloat16 [1024, 153], replicated, may hold values from -0.1875 to 0.1875
Outputs:
- losses: float32 [16, 16], P('dp', 'cuts')
- grad_first_self: float32 [768, 1024], P('cuts')
- grad_first_neigh: float32 [768, 1024], P('cuts')
- grad_second_self: float32 [1024, 1024], P('cuts')
- grad_second_neigh: float32 [1024, 1024], P('cuts')
- grad_third_self: float32 [1024, 153], P('cuts')
- grad_third_neigh: float32 [1024, 153], P('cuts')
The draws below stay inside these ranges and needn't reach their ends.
All inputs are finite; a program needn't handle non-finite values.
Results may differ from the reference program's by a relative error of at most 0.024.
Values may be sent and summed in bfloat16 or wider, within the bound.
A program may use at most 128 MiB of HBM per device.

```python
import jax
import jax.numpy as jnp
from jax import lax

F = 768
HID = 1024
CLASSES = 153
SEEDS = 128
FAN1 = 5
FAN2 = 5
FAN3 = 3
R2 = 160
R1 = 192
R0 = 1024
GROUPS = 16
MBG = 16


def set_ends(values, stream_key, smallest, top_value):
    place = [jax.random.randint(jax.random.fold_in(stream_key, axis), (), 0, length) for axis, length in enumerate(values.shape)]
    main_axis = values.shape.index(max(values.shape))
    neighbour = place[:main_axis] + [(place[main_axis] + 1) % values.shape[main_axis]] + place[main_axis + 1:]
    return values.at[tuple(place)].set(smallest).at[tuple(neighbour)].set(top_value)


def level_of(own_key, dims, pieces, least, high):
    def one(position, parts):
        draws = jax.random.uniform(jax.random.fold_in(jax.random.fold_in(own_key, 6), position), (parts,), jnp.float32, least / len(pieces), high / len(pieces))
        return jnp.repeat(jnp.exp(draws), dims[position] // parts).reshape((-1,) + (1,) * (len(dims) - position - 1))

    factor_of = one(*pieces[0])
    for cut in pieces[1:]:
        factor_of = factor_of * one(*cut)
    return factor_of


def centred(stream_key, extent, scale, most, pieces=(), kind=jnp.bfloat16):
    values = scale * jax.random.normal(stream_key, extent, jnp.float32)
    if pieces:
        values = values * level_of(stream_key, extent, pieces, -0.22, 0.18)
    return jnp.clip(values, -most, most).astype(kind)


def setup_inputs(seed: int = 0) -> dict:
    key_of = jax.random.split(jax.random.key(seed), 12)
    features = centred(key_of[0], (GROUPS, MBG, R0, F), 1.0, 6.0, ((0, 16), (3, 16)))
    lists_one = set_ends(jax.random.randint(key_of[1], (GROUPS, MBG, R1, FAN1), 0, R0), jax.random.fold_in(key_of[1], 1), 0, R0 - 1).astype(jnp.int32)
    lists_two = set_ends(jax.random.randint(key_of[2], (GROUPS, MBG, R2, FAN2), 0, R1), jax.random.fold_in(key_of[2], 1), 0, R1 - 1).astype(jnp.int32)
    lists_three = set_ends(jax.random.randint(key_of[3], (GROUPS, MBG, SEEDS, FAN3), 0, R2), jax.random.fold_in(key_of[3], 1), 0, R2 - 1).astype(jnp.int32)
    labels = set_ends(jax.random.randint(key_of[4], (GROUPS, MBG, SEEDS), 0, CLASSES), jax.random.fold_in(key_of[4], 1), 0, CLASSES - 1).astype(jnp.int32)
    initial_node_weight = centred(key_of[5], (F, HID), F ** -0.5, 0.21875, ((0, 16),))
    initial_neighbour_weight = centred(key_of[6], (F, HID), F ** -0.5, 0.21875, ((0, 16),))
    second_self = centred(key_of[7], (HID, HID), HID ** -0.5, 0.1875)
    second_neigh = centred(key_of[8], (HID, HID), HID ** -0.5, 0.1875)
    final_node_weight = centred(key_of[9], (HID, CLASSES), HID ** -0.5, 0.1875)
    third_neigh = centred(key_of[10], (HID, CLASSES), HID ** -0.5, 0.1875)
    return {"features": features, "lists_one": lists_one, "lists_two": lists_two, "lists_three": lists_three, "labels": labels, "initial_node_weight": initial_node_weight, "initial_neighbour_weight": initial_neighbour_weight, "second_self": second_self, "second_neigh": second_neigh, "final_node_weight": final_node_weight, "third_neigh": third_neigh}


def counting(indices, columns):
    hits = indices[:, :, None] == jnp.arange(columns, dtype=jnp.int32)[None, None, :]
    return jnp.sum(hits.astype(jnp.float32), axis=1).astype(jnp.bfloat16)


def aggregate(counts, source, fanout):
    summed = jnp.dot(counts, source, preferred_element_type=jnp.float32)
    return (summed * (1.0 / fanout)).astype(jnp.bfloat16)


def activate(values):
    return values * jax.nn.sigmoid(values)


def slope(values):
    sigma = jax.nn.sigmoid(values)
    return sigma * (1.0 + values * (1.0 - sigma))


def upper_layers(pre_one, lists_two, lists_three, seed_labels, second_self, second_neigh, final_node_weight, third_neigh):
    rows_one = pre_one.shape[0]
    rows_two = lists_two.shape[0]
    seed_count = lists_three.shape[0]
    act_one = activate(pre_one).astype(jnp.bfloat16)
    counts_two = counting(lists_two, rows_one)
    mean_two = aggregate(counts_two, act_one, FAN2)
    pre_two = jnp.dot(act_one[:rows_two], second_self, preferred_element_type=jnp.float32) + jnp.dot(mean_two, second_neigh, preferred_element_type=jnp.float32)
    act_two = activate(pre_two).astype(jnp.bfloat16)
    counts_three = counting(lists_three, rows_two)
    mean_three = aggregate(counts_three, act_two, FAN3)
    logits = jnp.dot(act_two[:seed_count], final_node_weight, preferred_element_type=jnp.float32) + jnp.dot(mean_three, third_neigh, preferred_element_type=jnp.float32)
    expon = jnp.exp(logits)
    combined_sums = jnp.sum(expon, axis=1, keepdims=True)
    onehot_labels = (seed_labels[:, None] == jnp.arange(logits.shape[1], dtype=jnp.int32)[None, :]).astype(jnp.float32)
    mean_loss = jnp.mean(jnp.log(combined_sums[:, 0]) - jnp.sum(logits * onehot_labels, axis=1))
    grad_logits = ((expon / combined_sums - onehot_labels) * (1.0 / seed_count)).astype(jnp.bfloat16)
    grad_third_self = jnp.dot(act_two[:seed_count].T, grad_logits, preferred_element_type=jnp.float32)
    grad_third_neigh = jnp.dot(mean_three.T, grad_logits, preferred_element_type=jnp.float32)
    back_three = (jnp.dot(grad_logits, third_neigh.T, preferred_element_type=jnp.float32) * (1.0 / FAN3)).astype(jnp.bfloat16)
    own_three = jnp.dot(grad_logits, final_node_weight.T, preferred_element_type=jnp.float32)
    grad_act_two = jnp.pad(own_three, ((0, rows_two - seed_count), (0, 0))) + jnp.dot(counts_three.T, back_three, preferred_element_type=jnp.float32)
    grad_pre_two = (grad_act_two * slope(pre_two)).astype(jnp.bfloat16)
    grad_second_self = jnp.dot(act_one[:rows_two].T, grad_pre_two, preferred_element_type=jnp.float32)
    grad_second_neigh = jnp.dot(mean_two.T, grad_pre_two, preferred_element_type=jnp.float32)
    back_two = (jnp.dot(grad_pre_two, second_neigh.T, preferred_element_type=jnp.float32) * (1.0 / FAN2)).astype(jnp.bfloat16)
    own_two = jnp.dot(grad_pre_two, second_self.T, preferred_element_type=jnp.float32)
    grad_act_one = jnp.pad(own_two, ((0, rows_one - rows_two), (0, 0))) + jnp.dot(counts_two.T, back_two, preferred_element_type=jnp.float32)
    grad_pre_one = (grad_act_one * slope(pre_one)).astype(jnp.bfloat16)
    return mean_loss, (grad_second_self, grad_second_neigh, grad_third_self, grad_third_neigh), grad_pre_one


def reference(features, lists_one, lists_two, lists_three, labels, initial_node_weight, initial_neighbour_weight, second_self, second_neigh, final_node_weight, third_neigh):
    batches = GROUPS * MBG
    flat = (features.reshape(batches, R0, F), lists_one.reshape(batches, R1, FAN1), lists_two.reshape(batches, R2, FAN2), lists_three.reshape(batches, SEEDS, FAN3), labels.reshape(batches, SEEDS))

    def visit(running, item):
        frontier, first_lists, second_lists, third_lists, seed_labels = item
        counts_one = counting(first_lists, R0)
        mean_one = aggregate(counts_one, frontier, FAN1)
        pre_one = jnp.dot(frontier[:R1], initial_node_weight, preferred_element_type=jnp.float32) + jnp.dot(mean_one, initial_neighbour_weight, preferred_element_type=jnp.float32)
        mean_loss, upper_grads, grad_pre_one = upper_layers(pre_one, second_lists, third_lists, seed_labels, second_self, second_neigh, final_node_weight, third_neigh)
        grad_self = jnp.dot(frontier[:R1].T, grad_pre_one, preferred_element_type=jnp.float32)
        grad_neigh = jnp.dot(mean_one.T, grad_pre_one, preferred_element_type=jnp.float32)
        terms = (grad_self, grad_neigh) + upper_grads
        return tuple(left + right for left, right in zip(running, terms)), mean_loss

    initial_partial_sums = (jnp.zeros((F, HID), jnp.float32), jnp.zeros((F, HID), jnp.float32), jnp.zeros((HID, HID), jnp.float32), jnp.zeros((HID, HID), jnp.float32), jnp.zeros((HID, CLASSES), jnp.float32), jnp.zeros((HID, CLASSES), jnp.float32))
    running, mean_losses = lax.scan(visit, initial_partial_sums, flat)
    return mean_losses.reshape(GROUPS, MBG), running[0], running[1], running[2], running[3], running[4], running[5]
```

```python
import jax
import jax.numpy as jnp
from jax import lax
from jax.experimental import pallas as pl
from jax.experimental.pallas import tpu as pltpu
from jax.sharding import PartitionSpec as P

MESH = pl.DeviceIdType.MESH
BF = jnp.bfloat16
F32 = jnp.float32
FAN1 = 5
FAN2 = 5
FAN3 = 3
R0 = 1024
R1 = 192
R2 = 160
SEEDS = 128
HID = 1024
CUTS = 16
WIDE = 48
CLASSES = 153
PADDED = 256
VMEM = pl.BlockSpec(memory_space=pltpu.VMEM)


def place():
    d, c = lax.axis_index("dp"), lax.axis_index("cuts")
    return c // 4, d // 4, c % 4, (d // 2) % 2, d % 2


def device(x, y, zh, zl, k):
    return {"dp": (y * 2 + zl) * 2 + k, "cuts": x * 4 + zh}


def remote(src, dst, send, recv, to):
    return pltpu.make_async_remote_copy(
        src_ref=src, dst_ref=dst, send_sem=send, recv_sem=recv, device_id=to, device_id_type=MESH
    )


def gather_kernel(
    lists, xt, w_self, w_neigh, at, w,
    blk_out, blk_in, half,
    a_send, a_recv, wz_send, wz_recv, wx_send, wx_recv, wk_send, wk_recv,
):
    x, y, zh, zl, k = place()
    me = x * 4 + zh
    sibling = device(x, y, zh, zl, 1 - k)

    barrier = pltpu.get_barrier_semaphore()
    for s in range(1, CUTS):
        pl.semaphore_signal(
            barrier, 1, device_id={"dp": lax.axis_index("dp"), "cuts": (me + s) % CUTS},
            device_id_type=MESH,
        )
    pl.semaphore_signal(barrier, 1, device_id=sibling, device_id_type=MESH)
    pl.semaphore_wait(barrier, CUTS)

    half[...] = jnp.where(k == 0, w_self[...], w_neigh[...])
    w[0, me] = w_self[...]
    w[1, me] = w_neigh[...]
    sends = []
    for s in range(1, 4):
        cp = remote(
            half, w.at[k, me], wz_send.at[s - 1], wz_recv.at[s - 1],
            device(x, y, (zh + s) % 4, zl, k),
        )
        cp.start()
        sends.append(cp)

    def spread_x(j):
        src = x * 4 + (zh + 4 - j) % 4
        for s in range(1, 4):
            n = j * 3 + s - 1
            cp = remote(
                w.at[k, src] if j else half, w.at[k, src], wx_send.at[n], wx_recv.at[n],
                device((x + s) % 4, y, zh, zl, k),
            )
            cp.start()
            sends.append(cp)

    def spread_core(n, src):
        cp = remote(w.at[k, src], w.at[k, src], wk_send.at[n], wk_recv.at[n], sibling)
        cp.start()
        sends.append(cp)

    spread_x(0)

    def block(m):
        idx = lists[:, pl.ds(m, 1), :]
        rows = lax.broadcasted_iota(jnp.int32, (R0, R1), 0)
        counts = jnp.zeros((R0, R1), F32)
        for f in range(FAN1):
            counts = counts + jnp.where(rows == idx[f], 1.0, 0.0)
        mean = jnp.dot(xt[m], counts.astype(BF), preferred_element_type=F32)
        mean = (mean * (1.0 / FAN1)).astype(BF)
        own = xt[m][:, :R1]
        return own, mean

    def pack(ref, m, own, mean):
        ref[m, 0:48] = own[:, 0:128]
        ref[m, 48:96] = mean[:, 0:128]
        ref[m, 96:144] = jnp.concatenate([own[:, 128:192], mean[:, 128:192]], axis=1)

    def a_copy(s):
        m = (me + s) % CUTS
        return remote(
            blk_out.at[m], blk_in.at[me], a_send.at[s - 1], a_recv.at[s - 1],
            {"dp": lax.axis_index("dp"), "cuts": m},
        )

    def one(s, _):
        m = (me + s) % CUTS
        own, mean = block(m)
        pack(blk_out, m, own, mean)
        a_copy(s).start()
        return 0

    def z_arrival(j):
        remote(
            half, w.at[k, x * 4 + (zh + 4 - j) % 4], wz_send.at[j - 1], wz_recv.at[j - 1], sibling
        ).wait_recv()
        spread_x(j)
        spread_core(j - 1, x * 4 + (zh + 4 - j) % 4)

    lax.fori_loop(1, 6, one, 0)
    z_arrival(1)
    lax.fori_loop(6, 9, one, 0)
    z_arrival(3)
    lax.fori_loop(9, 12, one, 0)
    z_arrival(2)
    lax.fori_loop(12, 16, one, 0)
    own, mean = block(me)
    pack(blk_in, me, own, mean)

    for j in (0, 1, 3, 2):
        for s in range(1, 4):
            n = j * 3 + s - 1
            src = ((x + 4 - s) % 4) * 4 + (zh + 4 - j) % 4
            remote(half, w.at[k, src], wx_send.at[n], wx_recv.at[n], sibling).wait_recv()
            spread_core(3 + n, src)

    for s in range(1, CUTS):
        frm = (me + CUTS - s) % CUTS
        remote(blk_out.at[frm], blk_in.at[frm], a_send.at[s - 1], a_recv.at[s - 1], sibling).wait_recv()
    for c in range(CUTS):
        tail = blk_in[c, 96:144]
        at[0, c * 48:(c + 1) * 48, 0:128] = blk_in[c, 0:48]
        at[1, c * 48:(c + 1) * 48, 0:128] = blk_in[c, 48:96]
        at[0, c * 48:(c + 1) * 48, 128:192] = tail[:, 0:64]
        at[1, c * 48:(c + 1) * 48, 128:192] = tail[:, 64:128]

    for j in range(1, 4):
        remote(half, w.at[1 - k, x * 4 + (zh + 4 - j) % 4], wk_send.at[j - 1], wk_recv.at[j - 1], sibling).wait_recv()
    for j in range(4):
        for s in range(1, 4):
            n = j * 3 + s - 1
            src = ((x + 4 - s) % 4) * 4 + (zh + 4 - j) % 4
            remote(half, w.at[1 - k, src], wk_send.at[3 + n], wk_recv.at[3 + n], sibling).wait_recv()
    for cp in sends:
        cp.wait_send()

    def sent(s, _):
        a_copy(s).wait_send()
        return 0

    lax.fori_loop(1, CUTS, sent, 0)


def gather(lists, xt, w_self, w_neigh):
    dma = pltpu.SemaphoreType.DMA
    return pl.pallas_call(
        gather_kernel,
        out_shape=(
            jax.ShapeDtypeStruct((2, CUTS * WIDE, R1), BF),
            jax.ShapeDtypeStruct((2, CUTS, WIDE, HID), BF),
        ),
        in_specs=[VMEM] * 4,
        out_specs=(VMEM, VMEM),
        scratch_shapes=[
            pltpu.VMEM((CUTS, 144, 128), BF),
            pltpu.VMEM((CUTS, 144, 128), BF),
            pltpu.VMEM((WIDE, HID), BF),
            dma((15,)), dma((15,)), dma((3,)), dma((3,)), dma((12,)), dma((12,)), dma((15,)), dma((15,)),
        ],
        compiler_params=pltpu.CompilerParams(
            collective_id=1, has_side_effects=True, vmem_limit_bytes=48 * 2**20
        ),
    )(lists, xt, w_self, w_neigh)


def reduce_kernel(
    a1, a2, a3, g1, g2, g3, out,
    ra1, ra2, ra3, rg1, rg2, rg3,
    s_buf, r_one, r_x, t1, t2, r_two, u, r_z,
    c_send, c_recv, s1_send, s1_recv, s2_send, s2_recv, z_send, z_recv, f_send, f_recv, k_send, k_recv,
):
    x, y, zh, zl, k = place()
    sibling = device(x, y, zh, zl, 1 - k)
    xs = [(x + s) % 4 for s in range(4)]
    ys = [(y + s) % 4 for s in range(4)]
    zpos = zl * 4 + zh

    def z_peer(s):
        p = (zpos + s) % 8
        return p // 4, p % 4

    def f_peer(s):
        p = (y * 2 + zl + s) % 8
        return p // 2, p % 2

    barrier = pltpu.get_barrier_semaphore()
    peers = [sibling]
    peers += [device(xs[s], y, zh, zl, k) for s in range(1, 4)]
    for s in range(1, 8):
        pzl, pzh = z_peer(s)
        peers.append(device(x, y, pzh, pzl, k))
    for s in range(1, 8):
        py, pzl = f_peer(s)
        peers.append(device(x, py, zh, pzl, k))
    for p in peers:
        pl.semaphore_signal(barrier, 1, device_id=p, device_id_type=MESH)
    pl.semaphore_wait(barrier, len(peers))

    sends = []

    def go(cp):
        cp.start()
        sends.append(cp)

    pairs = ((a3.at[1 - k], ra3), (g3, rg3), (a2.at[1 - k], ra2), (g2, rg2), (a1.at[1 - k], ra1), (g1, rg1))
    swaps = []
    for i, (src, dst) in enumerate(pairs):
        cp = remote(src, dst, c_send.at[i], c_recv.at[i], sibling)
        go(cp)
        swaps.append(cp)

    def products(a_own, g_own, a_sib, g_sib, lanes):
        return (
            jnp.dot(a_own, g_own[:, lanes], preferred_element_type=F32)
            + jnp.dot(a_sib, g_sib[:, lanes], preferred_element_type=F32)
        ).astype(BF)

    swaps[0].wait_recv()
    swaps[1].wait_recv()
    third = products(a3[k].T, g3, ra3[...].T, rg3, slice(0, 256)).reshape(CUTS, 4, 16, 256)
    for j in range(4):
        s_buf[j // 2, 7, :, :, (j % 2) * 256:(j % 2 + 1) * 256] = third[:, j]
    swaps[2].wait_recv()
    swaps[3].wait_recv()
    a_own, a_sib = a2[k].T, ra2[...].T
    for n in range(4):
        p = products(a_own, g2, a_sib, rg2, slice(n * 256, (n + 1) * 256)).reshape(CUTS, 4, 16, 256)
        for g in range(4):
            s_buf[n // 2, 3 + g, :, :, (n % 2) * 256:(n % 2 + 1) * 256] = p[:, g]
    swaps[4].wait_recv()
    swaps[5].wait_recv()
    a_own, a_sib = a1[k], ra1[...]
    for n in range(4):
        p = products(a_own, g1, a_sib, rg1, slice(n * 256, (n + 1) * 256)).reshape(CUTS, 3, 16, 256)
        for g in range(3):
            s_buf[n // 2, g, :, :, (n % 2) * 256:(n % 2 + 1) * 256] = p[:, g]

    one = []
    for s in range(1, 4):
        cp = remote(
            s_buf.at[0, pl.ds(ys[s] * 2, 2)], r_one.at[s - 1], s1_send.at[s - 1], s1_recv.at[s - 1],
            device(x, ys[s], zh, zl, k),
        )
        go(cp)
        one.append(cp)
    for s in range(1, 4):
        cp = remote(
            s_buf.at[1, :, pl.ds(xs[s] * 4, 4)],
            r_x.at[s - 1],
            s1_send.at[s + 2], s1_recv.at[s + 2],
            device(xs[s], y, zh, zl, k),
        )
        go(cp)
        one.append(cp)
    for cp in one:
        cp.wait_recv()

    def add_y(c, _):
        for q in range(2):
            v = s_buf[0, y * 2 + q, c].astype(F32)
            for s in range(3):
                v = v + r_one[s, q, c].astype(F32)
            t1[q, c] = v.astype(BF)
        return 0

    lax.fori_loop(0, CUTS, add_y, 0)

    def add_x(g, _):
        for h in range(4):
            v = s_buf[1, g, x * 4 + h].astype(F32)
            for s in range(3):
                v = v + r_x[s, g, h].astype(F32)
            t2[g, h] = v.astype(BF)
        return 0

    lax.fori_loop(0, 8, add_x, 0)

    two = []
    for s in range(1, 4):
        cp = remote(
            t1.at[:, pl.ds(xs[s] * 4, 4)], r_two.at[0, s - 1], s2_send.at[s - 1], s2_recv.at[s - 1],
            device(xs[s], y, zh, zl, k),
        )
        go(cp)
        two.append(cp)
    for s in range(1, 4):
        cp = remote(
            t2.at[pl.ds(ys[s] * 2, 2)], r_two.at[1, s - 1], s2_send.at[s + 2], s2_recv.at[s + 2],
            device(x, ys[s], zh, zl, k),
        )
        go(cp)
        two.append(cp)
    for cp in two:
        cp.wait_recv()
    for q in range(2):
        for h in range(4):
            v = t1[q, x * 4 + h].astype(F32)
            for s in range(3):
                v = v + r_two[0, s, q, h].astype(F32)
            u[q, h, :, 0:512] = v.astype(BF)
            v = t2[y * 2 + q, h].astype(F32)
            for s in range(3):
                v = v + r_two[1, s, q, h].astype(F32)
            u[q, h, :, 512:1024] = v.astype(BF)

    zs = []
    for s in range(1, 8):
        pzl, pzh = z_peer(s)
        cp = remote(
            u.at[pzl, pzh], r_z.at[s - 1], z_send.at[s - 1], z_recv.at[s - 1], device(x, y, pzh, pzl, k)
        )
        go(cp)
        zs.append(cp)
    for cp in zs:
        cp.wait_recv()
    v = u[zl, zh].astype(F32)
    for s in range(7):
        v = v + r_z[s].astype(F32)
    mine = y * 2 + zl
    out[k, mine] = v.astype(BF)

    for s in range(1, 8):
        py, pzl = f_peer(s)
        go(remote(out.at[k, mine], out.at[k, mine], f_send.at[s - 1], f_recv.at[s - 1], device(x, py, zh, pzl, k)))
    for s in range(1, 8):
        frm = (mine + 8 - s) % 8
        remote(out.at[k, frm], out.at[k, frm], f_send.at[s - 1], f_recv.at[s - 1], sibling).wait_recv()
    last = remote(out.at[k], out.at[k], k_send.at[0], k_recv.at[0], sibling)
    go(last)
    remote(out.at[1 - k], out.at[1 - k], k_send.at[0], k_recv.at[0], sibling).wait_recv()
    for cp in sends:
        cp.wait_send()


def reduce_grads(a1, a2, a3, g1, g2, g3):
    dma = pltpu.SemaphoreType.DMA
    vm = lambda *shape: pltpu.VMEM(shape, BF)
    return pl.pallas_call(
        reduce_kernel,
        out_shape=jax.ShapeDtypeStruct((2, 8, 16, HID), BF),
        in_specs=[VMEM] * 6,
        out_specs=VMEM,
        scratch_shapes=[
            vm(CUTS * WIDE, R1), vm(R2, HID), vm(SEEDS, HID), vm(R1, HID), vm(R2, HID), vm(SEEDS, PADDED),
            vm(2, 8, CUTS, 16, 512),
            vm(3, 2, CUTS, 16, 512), vm(3, 8, 4, 16, 512),
            vm(2, CUTS, 16, 512),
            vm(8, 4, 16, 512),
            vm(2, 3, 2, 4, 16, 512),
            vm(2, 4, 16, HID),
            vm(7, 16, HID),
            dma((6,)), dma((6,)), dma((6,)), dma((6,)), dma((6,)), dma((6,)), dma((7,)), dma((7,)),
            dma((7,)), dma((7,)), dma((1,)), dma((1,)),
        ],
        compiler_params=pltpu.CompilerParams(
            collective_id=2, has_side_effects=True, vmem_limit_bytes=56 * 2**20
        ),
    )(a1, a2, a3, g1, g2, g3)


def finish_kernel(sums, first_self, first_neigh, second_self, second_neigh, third_self, third_neigh):
    for k, first, second, third in ((0, first_self, second_self, third_self), (1, first_neigh, second_neigh, third_neigh)):
        first[...] = sums[k, 0:3].reshape(48, HID).astype(F32)
        second[...] = sums[k, 3:7].reshape(64, HID).astype(F32)
        for j in range(4):
            third[j * 16:(j + 1) * 16] = sums[k, 7][:, j * 256:j * 256 + CLASSES].astype(F32)


def finish(sums):
    shapes = ((48, HID), (48, HID), (64, HID), (64, HID), (64, CLASSES), (64, CLASSES))
    return pl.pallas_call(
        finish_kernel,
        out_shape=tuple(jax.ShapeDtypeStruct(s, F32) for s in shapes),
        in_specs=[VMEM],
        out_specs=(VMEM,) * 6,
    )(sums)


def counting(indices, columns):
    hits = indices[:, :, None] == jnp.arange(columns, dtype=jnp.int32)[None, None, :]
    return jnp.sum(hits.astype(F32), axis=1).astype(BF)


def aggregate(counts, source, fanout):
    summed = jnp.dot(counts, source, preferred_element_type=F32)
    return (summed * (1.0 / fanout)).astype(BF)


def activate(values):
    return values * jax.nn.sigmoid(values)


def slope(values):
    sigma = jax.nn.sigmoid(values)
    return sigma * (1.0 + values * (1.0 - sigma))


def upper_layers(pre_one, lists_two, lists_three, seed_labels, second_self, second_neigh, final_node_weight, third_neigh):
    act_one = activate(pre_one).astype(BF)
    counts_two = counting(lists_two, R1)
    mean_two = aggregate(counts_two, act_one, FAN2)
    pre_two = jnp.dot(act_one[:R2], second_self, preferred_element_type=F32) + jnp.dot(
        mean_two, second_neigh, preferred_element_type=F32
    )
    act_two = activate(pre_two).astype(BF)
    counts_three = counting(lists_three, R2)
    mean_three = aggregate(counts_three, act_two, FAN3)
    logits = jnp.dot(act_two[:SEEDS], final_node_weight, preferred_element_type=F32) + jnp.dot(
        mean_three, third_neigh, preferred_element_type=F32
    )
    expon = jnp.exp(logits)
    sums = jnp.sum(expon, axis=1, keepdims=True)
    onehot = (seed_labels[:, None] == jnp.arange(CLASSES, dtype=jnp.int32)[None, :]).astype(F32)
    mean_loss = jnp.mean(jnp.log(sums[:, 0]) - jnp.sum(logits * onehot, axis=1))
    grad_logits = ((expon / sums - onehot) * (1.0 / SEEDS)).astype(BF)
    back_three = (jnp.dot(grad_logits, third_neigh.T, preferred_element_type=F32) * (1.0 / FAN3)).astype(BF)
    own_three = jnp.dot(grad_logits, final_node_weight.T, preferred_element_type=F32)
    grad_act_two = jnp.pad(own_three, ((0, R2 - SEEDS), (0, 0))) + jnp.dot(
        counts_three.T, back_three, preferred_element_type=F32
    )
    grad_pre_two = (grad_act_two * slope(pre_two)).astype(BF)
    back_two = (jnp.dot(grad_pre_two, second_neigh.T, preferred_element_type=F32) * (1.0 / FAN2)).astype(BF)
    own_two = jnp.dot(grad_pre_two, second_self.T, preferred_element_type=F32)
    grad_act_one = jnp.pad(own_two, ((0, R1 - R2), (0, 0))) + jnp.dot(
        counts_two.T, back_two, preferred_element_type=F32
    )
    grad_pre_one = (grad_act_one * slope(pre_one)).astype(BF)
    a2 = jnp.stack([act_one[:R2], mean_two])
    a3 = jnp.stack([act_two[:SEEDS], mean_three])
    g3 = jnp.pad(grad_logits, ((0, 0), (0, PADDED - CLASSES)))
    return mean_loss, a2, a3, grad_pre_one, grad_pre_two, g3


def per_device(
    features, lists_one, lists_two, lists_three, labels, initial_node_weight, initial_neighbour_weight,
    second_self, second_neigh, final_node_weight, third_neigh,
):
    xt = jnp.swapaxes(features[0], 1, 2)
    lists = jnp.transpose(lists_one[0], (2, 0, 1))
    at, w = gather(lists, xt, initial_node_weight, initial_neighbour_weight)
    pre_one = lax.dot_general(
        at.reshape(2 * CUTS * WIDE, R1), w.reshape(2 * CUTS * WIDE, HID), (((0,), (0,)), ((), ())),
        preferred_element_type=F32,
    )
    mean_loss, a2, a3, g1, g2, g3 = upper_layers(
        pre_one, lists_two[0, 0], lists_three[0, 0], labels[0, 0],
        second_self, second_neigh, final_node_weight, third_neigh,
    )
    sums = reduce_grads(at, a2, a3, g1, g2, g3)
    return (mean_loss.reshape(1, 1),) + tuple(finish(sums))


def solution(mesh):
    return jax.shard_map(
        per_device,
        mesh=mesh,
        in_specs=(
            P("dp", None, None, "cuts"),
            P("dp", None, None, None),
            P("dp", "cuts", None, None),
            P("dp", "cuts", None, None),
            P("dp", "cuts", None),
            P("cuts", None),
            P("cuts", None),
            P(), P(), P(), P(),
        ),
        out_specs=(P("dp", "cuts"),) + (P("cuts", None),) * 6,
        check_vma=False,
    )
```

```python
import jax
import jax.numpy as jnp
from jax import lax
from jax.experimental import pallas as pl
from jax.experimental.pallas import tpu as pltpu
from jax.sharding import PartitionSpec as P

MESH = pl.DeviceIdType.MESH
BF = jnp.bfloat16
F32 = jnp.float32
FAN1 = 5
FAN2 = 5
FAN3 = 3
R0 = 1024
R1 = 192
R2 = 160
SEEDS = 128
HID = 1024
CUTS = 16
WIDE = 48
ROWS = CUTS * WIDE
CLASSES = 153
PADDED = 256
VMEM = pl.BlockSpec(memory_space=pltpu.VMEM)
ANY = pl.BlockSpec(memory_space=pl.ANY)
SLOTS = 192
UPPER = (48, 32)
LOWER = (16, 32)


def dot(a, b):
    return jnp.dot(a, b, preferred_element_type=F32)


def dot_nt(a, b):
    return lax.dot_general(a, b, (((1,), (1,)), ((), ())), preferred_element_type=F32)


def sigmoid(v):
    return 1.0 / (1.0 + jnp.exp(-v))


def slope(v):
    s = sigmoid(v)
    return s * (1.0 + v * (1.0 - s))


def lanes(n, width=256):
    if isinstance(n, int):
        return slice(n * width, (n + 1) * width)
    return pl.ds(pl.multiple_of(n * width, width), width)


def kernel(
    lists_hbm, xt_hbm, w_self_hbm, w_neigh_hbm, second_self_hbm, second_neigh_hbm, final_hbm, third_hbm, idx,
    loss, out_a, out_b,
    lists, xt, w_in, second, raw, top,
    blk_out, blk_in, wa, wb, at,
    pre1, act1, mean2, pre2, act2, mean3, back2, g1, g2, g3,
    ra1, ra2, ra3, rg1, rg2, rg3,
    *rest,
):
    bufs_a, bufs_b = rest[:13], rest[13:26]
    rest_keep, rest_rz = rest[26:30], rest[30:32]
    load, send, recv, a_send, a_recv = rest[32:]
    d, c = lax.axis_index("dp"), lax.axis_index("cuts")
    x, y, zh, zl, k = c // 4, d // 4, c % 4, (d // 2) % 2, d % 2
    me = c

    def device(px, py, pzh, pzl, pk):
        return {"dp": (py * 2 + pzl) * 2 + pk, "cuts": px * 4 + pzh}

    def peer(dx=0, dy=0, dzh=0, dzl=0, dk=0):
        return device((x + dx) % 4, (y + dy) % 4, (zh + dzh) % 4, (zl + dzl) % 2, (k + dk) % 2)

    sibling = peer(dk=1)
    xs = [(x + s) % 4 for s in range(4)]
    ys = [(y + s) % 4 for s in range(4)]

    barrier = pltpu.get_barrier_semaphore()
    peers = [peer(dx=s // 4, dzh=s % 4) for s in range(1, 16)]
    peers += [peer(dy=s // 2, dzl=s % 2) for s in range(1, 8)]
    peers += [peer(dzh=s, dzl=1) for s in range(1, 4)]
    peers += [sibling]
    for p in peers:
        pl.semaphore_signal(barrier, 1, device_id=p, device_id_type=MESH)

    count = [0]

    def fetch(src, dst):
        cp = pltpu.make_async_copy(src, dst, load.at[count[0]])
        count[0] += 1
        cp.start()
        return cp

    ld_lists = fetch(lists_hbm, lists)
    ld_w = [fetch(w_self_hbm, w_in.at[0]), fetch(w_neigh_hbm, w_in.at[1])]

    def xt_copy(s):
        m = (me + s) % CUTS
        return pltpu.make_async_copy(xt_hbm.at[m], xt.at[m], load.at[16 + s])

    def xt_start(s, _):
        xt_copy(s).start()
        return 0

    lax.fori_loop(1, CUTS + 1, xt_start, 0)
    ld_top = [fetch(final_hbm, raw.at[0]), fetch(third_hbm, raw.at[1])]
    ld_second = [fetch(second_self_hbm, second.at[0]), fetch(second_neigh_hbm, second.at[1])]

    sends = []

    def link(src, dst, to):
        n = len(sends)
        cp = pltpu.make_async_remote_copy(
            src_ref=src, dst_ref=dst, send_sem=send.at[n], recv_sem=recv.at[n], device_id=to, device_id_type=MESH
        )
        cp.start()
        sends.append(cp)
        return n

    def arrived(n, dst):
        pltpu.make_async_remote_copy(
            src_ref=dst, dst_ref=dst, send_sem=send.at[n], recv_sem=recv.at[n], device_id=sibling, device_id_type=MESH
        ).wait_recv()

    for cp in ld_w:
        cp.wait()
    for kk in range(2):
        wa[kk, me] = w_in[kk, :, 0:512]
    wb[k, y, me] = w_in[k, :, pl.ds(pl.multiple_of(512 + y * 128, 128), 128)]
    ld_lists.wait()
    pl.semaphore_wait(barrier, len(peers))

    wz = [
        (link(wa.at[k, me], wa.at[k, me], peer(dzh=s)), link(wb.at[k, y, me], wb.at[k, y, me], peer(dzh=s)))
        for s in range(1, 4)
    ]

    def spread_x(j):
        src = x * 4 + (zh + 4 - j) % 4
        return [link(wa.at[k, src], wa.at[k, src], peer(dx=s)) for s in range(1, 4)]

    wx = {0: spread_x(0)}
    wk = {}

    def spread_core(key, src):
        wk[key] = link(wa.at[k, src], wa.at[k, src], sibling)

    def block(m):
        rows = lax.broadcasted_iota(jnp.int32, (R0, R1), 0)
        counts = jnp.zeros((R0, R1), F32)
        for f in range(FAN1):
            counts = counts + jnp.where(rows == lists[f, pl.ds(m, 1), :], 1.0, 0.0)
        mean = (dot(xt[m], counts.astype(BF)) * (1.0 / FAN1)).astype(BF)
        return xt[m][:, :R1], mean

    def pack(ref, m, own, mean):
        ref[m, 0:48] = own[:, 0:128]
        ref[m, 48:96] = mean[:, 0:128]
        ref[m, 96:144] = jnp.concatenate([own[:, 128:192], mean[:, 128:192]], axis=1)

    def a_copy(s):
        m = (me + s) % CUTS
        return pltpu.make_async_remote_copy(
            src_ref=blk_out.at[m], dst_ref=blk_in.at[me], send_sem=a_send.at[s - 1], recv_sem=a_recv.at[s - 1],
            device_id={"dp": d, "cuts": m}, device_id_type=MESH,
        )

    def one(s, _):
        m = (me + s) % CUTS
        xt_copy(s).wait()
        own, mean = block(m)
        pack(blk_out, m, own, mean)
        a_copy(s).start()
        return 0

    def z_arrival(j):
        src = x * 4 + (zh + 4 - j) % 4
        arrived(wz[j - 1][0], wa.at[k, src])
        arrived(wz[j - 1][1], wb.at[k, y, src])
        wx[j] = spread_x(j)

    def mine_x(dx):
        return pl.ds(pl.multiple_of(((x + 4 + dx) % 4) * 4, 4), 4)

    lax.fori_loop(1, 5, one, 0)
    for j in (1, 3, 2):
        z_arrival(j)
    wbx = [link(wb.at[k, y, mine_x(0)], wb.at[k, y, mine_x(0)], peer(dx=s)) for s in range(1, 4)]
    for j in (1, 3, 2):
        spread_core((j, 0), x * 4 + (zh + 4 - j) % 4)
    lax.fori_loop(5, 10, one, 0)
    for s in range(1, 4):
        arrived(wbx[s - 1], wb.at[k, y, mine_x(-s)])
    wby = [link(wb.at[k, y], wb.at[k, y], peer(dy=s)) for s in range(1, 4)]
    wbk = {0: link(wb.at[k, y], wb.at[k, y], sibling)}
    lax.fori_loop(10, 16, one, 0)
    xt_copy(16).wait()
    own, mean = block(me)
    pack(blk_in, me, own, mean)

    for cp in ld_top:
        cp.wait()
    for i in range(2):
        top[i, 144:256] = jnp.zeros((112, HID), BF)
        top[i, 0:CLASSES] = raw[i]
    rows256 = lax.broadcasted_iota(jnp.int32, (256, 256), 0)

    def counting(first, fan):
        counts = jnp.zeros((256, 256), F32)
        for f in range(first, first + fan):
            counts = counts + jnp.where(rows256 == idx[f:f + 1, :], 1.0, 0.0)
        return counts

    counts2t, counts3t = counting(0, FAN2), counting(FAN2, FAN3)
    counts2, counts3 = counts2t.T.astype(BF), counts3t.T.astype(BF)
    counts2t, counts3t = counts2t.astype(BF), counts3t.astype(BF)
    onehot = jnp.where(rows256 == idx[8:9, :], 1.0, 0.0).T[:SEEDS]
    act1[R1:256] = jnp.zeros((256 - R1, HID), BF)
    act2[R2:256] = jnp.zeros((256 - R2, HID), BF)
    back2[R2:256] = jnp.zeros((256 - R2, HID), BF)

    for j in (0, 1, 3, 2):
        for s in range(1, 4):
            src = ((x + 4 - s) % 4) * 4 + (zh + 4 - j) % 4
            arrived(wx[j][s - 1], wa.at[k, src])
            spread_core((j, s), src)
    for s in range(1, CUTS):
        frm = (me + CUTS - s) % CUTS
        pltpu.make_async_remote_copy(
            src_ref=blk_in.at[frm], dst_ref=blk_in.at[frm], send_sem=a_send.at[s - 1], recv_sem=a_recv.at[s - 1],
            device_id=sibling, device_id_type=MESH,
        ).wait_recv()
    for i in range(CUTS):
        tail = blk_in[i, 96:144]
        at[0, i * 48:(i + 1) * 48, 0:128] = blk_in[i, 0:48]
        at[1, i * 48:(i + 1) * 48, 0:128] = blk_in[i, 48:96]
        at[0, i * 48:(i + 1) * 48, 128:192] = tail[:, 0:64]
        at[1, i * 48:(i + 1) * 48, 128:192] = tail[:, 64:128]
    sw_a1 = link(at.at[1 - k], ra1, sibling)
    at0, at1 = at[0].T, at[1].T
    for s in range(1, 4):
        frm = (y + 4 - s) % 4
        arrived(wby[s - 1], wb.at[k, frm])
        wbk[s] = link(wb.at[k, frm], wb.at[k, frm], sibling)
    for (j, s), n in wk.items():
        arrived(n, wa.at[1 - k, ((x + 4 - s) % 4) * 4 + (zh + 4 - j) % 4])
    for s in range(4):
        arrived(wbk[s], wb.at[1 - k, (y + 4 - s) % 4])

    for n in range(4):
        if n < 2:
            w0, w1 = (wa[i, :, :, lanes(n)].reshape(ROWS, 256) for i in range(2))
        else:
            q = 2 * n - 4
            w0, w1 = (
                jnp.concatenate([wb[i, q].reshape(ROWS, 128), wb[i, q + 1].reshape(ROWS, 128)], axis=1)
                for i in range(2)
            )
        v = dot(at0, w0) + dot(at1, w1)
        pre1[:, lanes(n)] = v
        act1[0:R1, lanes(n)] = (v * sigmoid(v)).astype(BF)
    for n in range(4):
        mean2[:, lanes(n)] = (dot(counts2[:R2], act1[:, lanes(n)]) * (1.0 / FAN2)).astype(BF)
    for cp in ld_second:
        cp.wait()
    for n in range(4):
        v = dot(act1[0:R2], second[0, :, lanes(n)]) + dot(mean2[...], second[1, :, lanes(n)])
        pre2[:, lanes(n)] = v
        act2[0:R2, lanes(n)] = (v * sigmoid(v)).astype(BF)
    for n in range(4):
        mean3[:, lanes(n)] = (dot(counts3[:SEEDS], act2[:, lanes(n)]) * (1.0 / FAN3)).astype(BF)
    logits = dot_nt(act2[0:SEEDS], top[0]) + dot_nt(mean3[...], top[1])
    column = lax.broadcasted_iota(jnp.int32, (SEEDS, PADDED), 1)
    expon = jnp.where(column < CLASSES, jnp.exp(logits), 0.0)
    total = jnp.sum(expon, axis=1, keepdims=True)
    each = jnp.log(total) - jnp.sum(logits * onehot, axis=1, keepdims=True)
    loss[...] = jnp.sum(each, axis=0, keepdims=True) * (1.0 / SEEDS)
    g3[...] = ((expon / total - onehot) * (1.0 / SEEDS)).astype(BF)

    sw_g3 = link(g3, rg3, sibling)
    keep3, keep2, give3, give2 = rest_keep
    give3[...] = jnp.where(k == 0, mean3[...], act2[0:SEEDS])
    keep3[...] = jnp.where(k == 0, act2[0:SEEDS], mean3[...])
    sw_a3 = link(give3, ra3, sibling)
    give2[...] = jnp.where(k == 0, mean2[...], act1[0:R2])
    keep2[...] = jnp.where(k == 0, act1[0:R2], mean2[...])
    sw_a2 = link(give2, ra2, sibling)
    for n in range(4):
        back = (dot(g3[...], top[1, :, lanes(n)]) * (1.0 / FAN3)).astype(BF)
        own = dot(g3[...], top[0, :, lanes(n)])
        grad = dot(counts3t[:R2, :SEEDS], back) + jnp.concatenate([own, jnp.zeros((R2 - SEEDS, 256), F32)], axis=0)
        g2[:, lanes(n)] = (grad * slope(pre2[:, lanes(n)])).astype(BF)
    sw_g2 = link(g2, rg2, sibling)

    class Ring:
        def __init__(self, block, add, up, down, relay, direct, comb):
            self.block, self.add, self.up, self.down = block, add, up, down
            self.relay, self.direct, self.comb = relay, direct, comb

        def opposite(self):
            self.n_relay = (
                link(self.block(2, 0), self.relay.at[0], self.up), link(self.block(2, 1), self.relay.at[1], self.down)
            )

        def to_up(self):
            self.n_up = link(self.block(1, 1), self.direct.at[1], self.up)

        def to_down(self):
            self.n_down = link(self.block(3, 0), self.direct.at[0], self.down)

        def pass_on(self):
            self.n_comb = []
            for h, off, to in ((0, 1, self.up), (1, 3, self.down)):
                arrived(self.n_relay[h], self.relay.at[h])
                self.add(self.relay.at[h], (self.relay.at[h], self.block(off, h)))
                self.n_comb.append(link(self.relay.at[h], self.comb.at[h], to))

        def finish(self, out):
            for h, n in ((0, self.n_down), (1, self.n_up)):
                arrived(self.n_comb[h], self.comb.at[h])
                arrived(n, self.direct.at[h])
                self.add(out(h), (self.block(0, h), self.comb.at[h], self.direct.at[h]))

    def add_leading(dst, parts):
        def body(i, _):
            v = parts[0][i].astype(F32)
            for p in parts[1:]:
                v = v + p[i].astype(F32)
            dst[i] = v.astype(BF)
            return 0

        lax.fori_loop(0, dst.shape[0], body, 0)

    class Chunk:
        def __init__(self, sizes, bufs, out):
            self.rows, self.out = sizes, out
            (
                self.s1, self.s2, rel1, dir1, com1, rel2, dir2, com2, self.t1, self.t2, self.q1, self.q2, self.u,
            ) = bufs[:13]
            self.y = Ring(
                lambda off, h: self.s1.at[ys[off], pl.ds(8 * h, 8)], add_leading, peer(dy=1), peer(dy=3), rel1, dir1, com1
            )
            self.x = Ring(
                lambda off, h: self.s2.at[:, pl.ds(xs[off] * 4 + 2 * h, 2)],
                add_leading, peer(dx=1), peer(dx=3), rel2, dir2, com2,
            )

        def first_done(self):
            self.y.finish(lambda h: self.t1.at[pl.ds(8 * h, 8)])
            self.n1 = [link(self.t1.at[mine_x(s)], self.q1.at[s - 1], peer(dx=s)) for s in range(1, 4)]
            self.x.finish(lambda h: self.t2.at[:, pl.ds(2 * h, 2)])
            self.n2 = [link(self.t2.at[ys[s]], self.q2.at[s - 1], peer(dy=s)) for s in range(1, 4)]

        def second_done(self, rz):
            r1, r2 = self.rows
            for lo, hi, numbers, t, q in (
                (0, r1, self.n1, lambda h: self.t1[x * 4 + h], self.q1),
                (r1, r1 + r2, self.n2, lambda h: self.t2[y, h], self.q2),
            ):
                for s in range(3):
                    arrived(numbers[s], q.at[s])
                for h in range(4):
                    v = t(h).astype(F32)
                    for s in range(3):
                        v = v + q[s, h].astype(F32)
                    v = v.astype(BF)
                    self.u[0, h, lo:hi] = v[:, 0:128]
                    self.u[1, h, lo:hi] = v[:, 128:256]
            self.rz = rz
            self.n3 = []
            for s in range(1, 8):
                p = (zl * 4 + zh + s) % 8
                self.n3.append(link(self.u.at[p // 4, p % 4], rz.at[s - 1], device(x, y, p % 4, p // 4, k)))

        def third_done(self):
            v = self.u[zl, zh].astype(F32)
            for s in range(7):
                arrived(self.n3[s], self.rz.at[s])
                v = v + self.rz[s].astype(F32)
            self.mine = y * 2 + zl
            piece = self.out.at[k, self.mine]
            self.out[k, self.mine] = v.astype(BF)
            self.n4 = []
            for s in range(1, 8):
                p = (self.mine + s) % 8
                self.n4.append(link(piece, piece, device(x, p // 2, zh, p % 2, k)))

        def gathered(self):
            for s in range(1, 8):
                arrived(self.n4[s - 1], self.out.at[k, (self.mine + 8 - s) % 8])
            self.n5 = link(self.out.at[k], self.out.at[k], sibling)

        def done(self):
            arrived(self.n5, self.out.at[1 - k])

    upper, lower = Chunk(UPPER, bufs_a, out_a), Chunk(LOWER, bufs_b, out_b)
    order = (2, 1, 3, 0)

    arrived(sw_g3, rg3)
    arrived(sw_a3, ra3)
    third = (dot(keep3[...].T, g3[...]) + dot(ra3[...].T, rg3[...])).astype(BF).reshape(CUTS, 4, 16, 256)
    for j in range(4):
        upper.s2[j, :, 16:32] = third[:, j]
    keep_t = keep2[...].T
    arrived(sw_a2, ra2)
    sib_t = ra2[...].T
    arrived(sw_g2, rg2)
    for off in order:
        n = ys[off]
        p = (dot(keep_t, g2[:, lanes(n)]) + dot(sib_t, rg2[:, lanes(n)])).astype(BF).reshape(CUTS, 64, 256)
        upper.s1[n] = p[:, 0:48]
        upper.s2[n, :, 0:16] = p[:, 48:64]
        if off == 2:
            upper.y.opposite()
        if off == 1:
            upper.y.to_up()
        if off == 3:
            upper.y.to_down()
    upper.x.opposite()
    upper.x.to_up()
    upper.x.to_down()

    for n in range(4):
        back2[0:R2, lanes(n)] = (dot_nt(g2[...], second[1, lanes(n), :]) * (1.0 / FAN2)).astype(BF)
    for n in range(4):
        own = dot_nt(g2[...], second[0, lanes(n), :])
        grad = dot(counts2t[:R1], back2[:, lanes(n)]) + jnp.concatenate(
            [own, jnp.zeros((R1 - R2, 256), F32)], axis=0
        )
        g1[:, lanes(n)] = (grad * slope(pre1[:, lanes(n)])).astype(BF)
    sw_g1 = link(g1, rg1, sibling)
    upper.y.pass_on()
    arrived(sw_a1, ra1)
    arrived(sw_g1, rg1)
    for off in order:
        n = ys[off]
        p = (dot(at[k], g1[:, lanes(n)]) + dot(ra1[...], rg1[:, lanes(n)])).astype(BF).reshape(CUTS, 48, 256)
        lower.s1[n] = p[:, 0:16]
        lower.s2[n] = p[:, 16:48]
        if off == 2:
            lower.y.opposite()
        if off == 1:
            lower.y.to_up()
            upper.x.pass_on()
        if off == 3:
            lower.y.to_down()
    lower.x.opposite()
    lower.x.to_up()
    lower.x.to_down()
    upper.first_done()
    lower.y.pass_on()
    lower.x.pass_on()
    upper.second_done(rest_rz[0])
    lower.first_done()
    upper.third_done()
    lower.second_done(rest_rz[1])
    upper.gathered()
    lower.third_done()
    lower.gathered()
    upper.done()
    lower.done()

    for cp in sends:
        cp.wait_send()

    def sent(s, _):
        a_copy(s).wait_send()
        return 0

    lax.fori_loop(1, CUTS, sent, 0)


def step(lists, xt, w_self, w_neigh, second_self, second_neigh, final_t, third_t, idx):
    dma = pltpu.SemaphoreType.DMA
    vm = lambda *shape: pltpu.VMEM(shape, BF)
    vf = lambda *shape: pltpu.VMEM(shape, F32)

    def chunk(sizes):
        r1, r2 = sizes
        return [
            vm(4, CUTS, r1, 256), vm(4, CUTS, r2, 256),
            vm(2, 8, r1, 256), vm(2, 8, r1, 256), vm(2, 8, r1, 256),
            vm(2, 4, 2, r2, 256), vm(2, 4, 2, r2, 256), vm(2, 4, 2, r2, 256),
            vm(CUTS, r1, 256), vm(4, 4, r2, 256),
            vm(3, 4, r1, 256), vm(3, 4, r2, 256),
            vm(2, 4, r1 + r2, 128),
        ]

    return pl.pallas_call(
        kernel,
        out_shape=(
            jax.ShapeDtypeStruct((1, 1), F32),
            jax.ShapeDtypeStruct((2, 8, sum(UPPER), 128), BF),
            jax.ShapeDtypeStruct((2, 8, sum(LOWER), 128), BF),
        ),
        in_specs=[ANY] * 8 + [VMEM],
        out_specs=(VMEM,) * 3,
        scratch_shapes=[
            pltpu.VMEM((FAN1, CUTS, R1), jnp.int32), vm(CUTS, WIDE, R0), vm(2, WIDE, HID), vm(2, HID, HID),
            vm(2, CLASSES, HID), vm(2, PADDED, HID),
            vm(CUTS, 144, 128), vm(CUTS, 144, 128), vm(2, CUTS, WIDE, 512), vm(2, 4, CUTS, WIDE, 128), vm(2, ROWS, R1),
            vf(R1, HID), vm(256, HID), vm(R2, HID), vf(R2, HID), vm(256, HID), vm(SEEDS, HID), vm(256, HID),
            vm(R1, HID), vm(R2, HID), vm(SEEDS, PADDED),
            vm(ROWS, R1), vm(R2, HID), vm(SEEDS, HID), vm(R1, HID), vm(R2, HID), vm(SEEDS, PADDED),
        ]
        + chunk(UPPER)
        + chunk(LOWER)
        + [
            vm(SEEDS, HID), vm(R2, HID), vm(SEEDS, HID), vm(R2, HID),
            vm(7, sum(UPPER), 128), vm(7, sum(LOWER), 128),
            dma((40,)), dma((SLOTS,)), dma((SLOTS,)), dma((15,)), dma((15,)),
        ],
        compiler_params=pltpu.CompilerParams(
            collective_id=1, has_side_effects=True, vmem_limit_bytes=56 * 2**20
        ),
    )(lists, xt, w_self, w_neigh, second_self, second_neigh, final_t, third_t, idx)


def finish_kernel(upper, lower, first_self, first_neigh, second_self, second_neigh, third_self, third_neigh):
    for k, first, second, third in (
        (0, first_self, second_self, third_self), (1, first_neigh, second_neigh, third_neigh)
    ):
        for g in range(8):
            first[:, lanes(g, 128)] = lower[k, g].astype(F32)
            second[:, lanes(g, 128)] = upper[k, g, 0:64].astype(F32)
            lo = (g % 2) * 128
            width = min(128, CLASSES - lo)
            third[g // 2 * 16:g // 2 * 16 + 16, lo:lo + width] = upper[k, g, 64:80, 0:width].astype(F32)


def finish(upper, lower):
    shapes = ((48, HID), (48, HID), (64, HID), (64, HID), (64, CLASSES), (64, CLASSES))
    return pl.pallas_call(
        finish_kernel,
        out_shape=tuple(jax.ShapeDtypeStruct(s, F32) for s in shapes),
        in_specs=[VMEM] * 2,
        out_specs=(VMEM,) * 6,
    )(upper, lower)


def per_device(
    features, lists_one, lists_two, lists_three, labels, initial_node_weight, initial_neighbour_weight,
    second_self, second_neigh, final_node_weight, third_neigh,
):
    xt = jnp.swapaxes(features[0], 1, 2)
    lists = jnp.transpose(lists_one[0], (2, 0, 1))

    def padded(v):
        return jnp.pad(v, ((0, 0), (0, 256 - v.shape[1])), constant_values=-1)

    idx = jnp.concatenate(
        [padded(lists_two[0, 0].T), padded(lists_three[0, 0].T), padded(labels[0]), jnp.full((7, 256), -1, jnp.int32)]
    )
    loss, upper, lower = step(
        lists, xt, initial_node_weight, initial_neighbour_weight, second_self, second_neigh,
        final_node_weight.T, third_neigh.T, idx,
    )
    return (loss,) + tuple(finish(upper, lower))


def solution(mesh):
    return jax.shard_map(
        per_device,
        mesh=mesh,
        in_specs=(
            P("dp", None, None, "cuts"),
            P("dp", None, None, None),
            P("dp", "cuts", None, None),
            P("dp", "cuts", None, None),
            P("dp", "cuts", None),
            P("cuts", None),
            P("cuts", None),
            P(), P(), P(), P(),
        ),
        out_specs=(P("dp", "cuts"),) + (P("cuts", None),) * 6,
        check_vma=False,
    )
```

```python
import jax
import jax.numpy as jnp
from jax import lax
from jax.experimental import pallas as pl
from jax.experimental.pallas import tpu as pltpu
from jax.sharding import PartitionSpec as P

MESH = pl.DeviceIdType.MESH
BF = jnp.bfloat16
F32 = jnp.float32
FAN1 = 5
FAN2 = 5
FAN3 = 3
R0 = 1024
R1 = 192
R2 = 160
SEEDS = 128
HID = 1024
CUTS = 16
WIDE = 48
ROWS = CUTS * WIDE
CLASSES = 153
PADDED = 256
VMEM = pl.BlockSpec(memory_space=pltpu.VMEM)
ANY = pl.BlockSpec(memory_space=pl.ANY)
SLOTS = 192
UPPER = (48, 32)
LOWER = (16, 32)


def dot(a, b):
    return jnp.dot(a, b, preferred_element_type=F32)


def dot_nt(a, b):
    return lax.dot_general(a, b, (((1,), (1,)), ((), ())), preferred_element_type=F32)


def sigmoid(v):
    return 1.0 / (1.0 + jnp.exp(-v))


def slope(v):
    s = sigmoid(v)
    return s * (1.0 + v * (1.0 - s))


def lanes(n, width=256):
    if isinstance(n, int):
        return slice(n * width, (n + 1) * width)
    return pl.ds(pl.multiple_of(n * width, width), width)


def kernel(
    lists_hbm, xt_hbm, w_self_hbm, w_neigh_hbm, second_self_hbm, second_neigh_hbm, final_hbm, third_hbm,
    lists2_hbm, lists3_hbm, labels_hbm,
    loss, out_a, out_b,
    lists, lists2, lists3, labels, idx, xt, w_in, second, raw, top,
    blk_out, blk_in, wa, wb, at,
    pre1, act1, mean2, pre2, act2, mean3, back2, g1, g2, g3,
    ra1, ra2, ra3, rg1, rg2, rg3,
    *rest,
):
    bufs_a, bufs_b = rest[:13], rest[13:26]
    rest_keep, rest_rz = rest[26:30], rest[30:32]
    load, send, recv, a_send, a_recv = rest[32:]
    d, c = lax.axis_index("dp"), lax.axis_index("cuts")
    x, y, zh, zl, k = c // 4, d // 4, c % 4, (d // 2) % 2, d % 2
    me = c

    def device(px, py, pzh, pzl, pk):
        return {"dp": (py * 2 + pzl) * 2 + pk, "cuts": px * 4 + pzh}

    def peer(dx=0, dy=0, dzh=0, dzl=0, dk=0):
        return device((x + dx) % 4, (y + dy) % 4, (zh + dzh) % 4, (zl + dzl) % 2, (k + dk) % 2)

    sibling = peer(dk=1)
    xs = [(x + s) % 4 for s in range(4)]
    ys = [(y + s) % 4 for s in range(4)]

    barrier = pltpu.get_barrier_semaphore()
    peers = [peer(dx=s // 4, dzh=s % 4) for s in range(1, 16)]
    peers += [peer(dy=s // 2, dzl=s % 2) for s in range(1, 8)]
    peers += [peer(dzh=s, dzl=1) for s in range(1, 4)]
    peers += [sibling]
    for p in peers:
        pl.semaphore_signal(barrier, 1, device_id=p, device_id_type=MESH)

    count = [0]

    def fetch(src, dst):
        cp = pltpu.make_async_copy(src, dst, load.at[count[0]])
        count[0] += 1
        cp.start()
        return cp

    ld_lists = fetch(lists_hbm, lists)
    ld_idx = [fetch(lists2_hbm, lists2), fetch(lists3_hbm, lists3), fetch(labels_hbm, labels)]
    ld_w = [fetch(w_self_hbm, w_in.at[0]), fetch(w_neigh_hbm, w_in.at[1])]

    def xt_copy(s):
        m = (me + s) % CUTS
        return pltpu.make_async_copy(xt_hbm.at[m], xt.at[m], load.at[16 + s])

    def xt_start(s, _):
        xt_copy(s).start()
        return 0

    lax.fori_loop(1, CUTS + 1, xt_start, 0)
    ld_top = [fetch(final_hbm, raw.at[0]), fetch(third_hbm, raw.at[1])]
    ld_second = [fetch(second_self_hbm, second.at[0]), fetch(second_neigh_hbm, second.at[1])]

    sends = []

    def link(src, dst, to):
        n = len(sends)
        cp = pltpu.make_async_remote_copy(
            src_ref=src, dst_ref=dst, send_sem=send.at[n], recv_sem=recv.at[n], device_id=to, device_id_type=MESH
        )
        cp.start()
        sends.append(cp)
        return n

    def arrived(n, dst):
        pltpu.make_async_remote_copy(
            src_ref=dst, dst_ref=dst, send_sem=send.at[n], recv_sem=recv.at[n], device_id=sibling, device_id_type=MESH
        ).wait_recv()

    for cp in ld_w:
        cp.wait()
    for kk in range(2):
        wa[kk, me] = w_in[kk, :, 0:512]
    wb[k, y, me] = w_in[k, :, pl.ds(pl.multiple_of(512 + y * 128, 128), 128)]
    ld_lists.wait()
    pl.semaphore_wait(barrier, len(peers))

    wbz = [link(wb.at[k, y, me], wb.at[k, y, me], peer(dzh=s)) for s in range(1, 4)]
    waz = [link(wa.at[k, me], wa.at[k, me], peer(dzh=s)) for s in range(1, 4)]

    def spread_x(j):
        src = x * 4 + (zh + 4 - j) % 4
        return [link(wa.at[k, src], wa.at[k, src], peer(dx=s)) for s in range(1, 4)]

    wx = {0: spread_x(0)}
    wk = {}

    def spread_core(key, src):
        wk[key] = link(wa.at[k, src], wa.at[k, src], sibling)

    def block(m):
        one, zero = jnp.ones((16, R1), BF), jnp.zeros((16, R1), BF)
        wanted = [jnp.broadcast_to(lists[f, pl.ds(m, 1), :], (16, R1)).astype(jnp.int16) for f in range(FAN1)]
        base = lax.broadcasted_iota(jnp.int32, (16, R1), 0).astype(jnp.int16)
        parts = []
        for b in range(R0 // 16):
            row = base + jnp.int16(16 * b)
            v = jnp.where(row == wanted[0], one, zero)
            for f in range(1, FAN1):
                v = v + jnp.where(row == wanted[f], one, zero)
            parts.append(v)
        mean = (dot(xt[m], jnp.concatenate(parts, axis=0)) * (1.0 / FAN1)).astype(BF)
        return xt[m][:, :R1], mean

    def pack(ref, m, own, mean):
        ref[m, 0:48] = own[:, 0:128]
        ref[m, 48:96] = mean[:, 0:128]
        ref[m, 96:144] = jnp.concatenate([own[:, 128:192], mean[:, 128:192]], axis=1)

    def a_copy(s):
        m = (me + s) % CUTS
        return pltpu.make_async_remote_copy(
            src_ref=blk_out.at[m], dst_ref=blk_in.at[me], send_sem=a_send.at[s - 1], recv_sem=a_recv.at[s - 1],
            device_id={"dp": d, "cuts": m}, device_id_type=MESH,
        )

    def one(s, _):
        m = (me + s) % CUTS
        xt_copy(s).wait()
        own, mean = block(m)
        pack(blk_out, m, own, mean)
        a_copy(s).start()
        return 0

    def behind(j):
        return x * 4 + (zh + 4 - j) % 4

    def z_arrival(j):
        arrived(waz[j - 1], wa.at[k, behind(j)])
        wx[j] = spread_x(j)
        spread_core((j, 0), behind(j))

    def mine_x(dx):
        return pl.ds(pl.multiple_of(((x + 4 + dx) % 4) * 4, 4), 4)

    lax.fori_loop(1, 5, one, 0)
    for j in range(1, 4):
        arrived(wbz[j - 1], wb.at[k, y, behind(j)])
    wbx = [link(wb.at[k, y, mine_x(0)], wb.at[k, y, mine_x(0)], peer(dx=s)) for s in range(1, 4)]
    lax.fori_loop(5, 8, one, 0)
    z_arrival(1)
    z_arrival(3)
    for s in range(1, 4):
        arrived(wbx[s - 1], wb.at[k, y, mine_x(-s)])
    wby = [link(wb.at[k, y], wb.at[k, y], peer(dy=s)) for s in range(1, 4)]
    wbk = {0: link(wb.at[k, y], wb.at[k, y], sibling)}
    z_arrival(2)
    lax.fori_loop(8, 16, one, 0)
    xt_copy(16).wait()
    own, mean = block(me)
    pack(blk_in, me, own, mean)

    for cp in ld_top:
        cp.wait()
    for i in range(2):
        top[i, 144:256] = jnp.zeros((112, HID), BF)
        top[i, 0:CLASSES] = raw[i]
    for cp in ld_idx:
        cp.wait()
    idx[...] = jnp.full((16, 256), -1, jnp.int32)
    for f in range(FAN2):
        idx[f:f + 1, 0:R2] = lists2[f]
    for f in range(FAN3):
        idx[FAN2 + f:FAN2 + f + 1, 0:SEEDS] = lists3[f]
    idx[8:9, 0:SEEDS] = labels[...]
    rows256 = lax.broadcasted_iota(jnp.int32, (256, 256), 0)

    def counting(first, fan):
        counts = jnp.zeros((256, 256), F32)
        for f in range(first, first + fan):
            counts = counts + jnp.where(rows256 == idx[f:f + 1, :], 1.0, 0.0)
        return counts

    counts2t, counts3t = counting(0, FAN2), counting(FAN2, FAN3)
    counts2, counts3 = counts2t.T.astype(BF), counts3t.T.astype(BF)
    counts2t, counts3t = counts2t.astype(BF), counts3t.astype(BF)
    onehot = jnp.where(rows256 == idx[8:9, :], 1.0, 0.0).T[:SEEDS]
    act1[R1:256] = jnp.zeros((256 - R1, HID), BF)
    act2[R2:256] = jnp.zeros((256 - R2, HID), BF)
    back2[R2:256] = jnp.zeros((256 - R2, HID), BF)

    for j in (0, 1, 3, 2):
        for s in range(1, 4):
            src = ((x + 4 - s) % 4) * 4 + (zh + 4 - j) % 4
            arrived(wx[j][s - 1], wa.at[k, src])
            spread_core((j, s), src)
    for s in range(1, CUTS):
        frm = (me + CUTS - s) % CUTS
        pltpu.make_async_remote_copy(
            src_ref=blk_in.at[frm], dst_ref=blk_in.at[frm], send_sem=a_send.at[s - 1], recv_sem=a_recv.at[s - 1],
            device_id=sibling, device_id_type=MESH,
        ).wait_recv()
    for i in range(CUTS):
        tail = blk_in[i, 96:144]
        at[0, i * 48:(i + 1) * 48, 0:128] = blk_in[i, 0:48]
        at[1, i * 48:(i + 1) * 48, 0:128] = blk_in[i, 48:96]
        at[0, i * 48:(i + 1) * 48, 128:192] = tail[:, 0:64]
        at[1, i * 48:(i + 1) * 48, 128:192] = tail[:, 64:128]
    sw_a1 = link(at.at[1 - k], ra1, sibling)
    at0, at1 = at[0].T, at[1].T
    for s in range(1, 4):
        frm = (y + 4 - s) % 4
        arrived(wby[s - 1], wb.at[k, frm])
        wbk[s] = link(wb.at[k, frm], wb.at[k, frm], sibling)

    for n in range(4):
        if n == 0:
            for (j, s), number in wk.items():
                arrived(number, wa.at[1 - k, ((x + 4 - s) % 4) * 4 + (zh + 4 - j) % 4])
        if n == 2:
            for s in range(4):
                arrived(wbk[s], wb.at[1 - k, (y + 4 - s) % 4])
        if n < 2:
            w0, w1 = (wa[i, :, :, lanes(n)].reshape(ROWS, 256) for i in range(2))
        else:
            q = 2 * n - 4
            w0, w1 = (
                jnp.concatenate([wb[i, q].reshape(ROWS, 128), wb[i, q + 1].reshape(ROWS, 128)], axis=1)
                for i in range(2)
            )
        v = dot(at0, w0) + dot(at1, w1)
        pre1[:, lanes(n)] = v
        act1[0:R1, lanes(n)] = (v * sigmoid(v)).astype(BF)
    for n in range(4):
        mean2[:, lanes(n)] = (dot(counts2[:R2], act1[:, lanes(n)]) * (1.0 / FAN2)).astype(BF)
    for cp in ld_second:
        cp.wait()
    for n in range(4):
        v = dot(act1[0:R2], second[0, :, lanes(n)]) + dot(mean2[...], second[1, :, lanes(n)])
        pre2[:, lanes(n)] = v
        act2[0:R2, lanes(n)] = (v * sigmoid(v)).astype(BF)
    for n in range(4):
        mean3[:, lanes(n)] = (dot(counts3[:SEEDS], act2[:, lanes(n)]) * (1.0 / FAN3)).astype(BF)
    logits = dot_nt(act2[0:SEEDS], top[0]) + dot_nt(mean3[...], top[1])
    column = lax.broadcasted_iota(jnp.int32, (SEEDS, PADDED), 1)
    expon = jnp.where(column < CLASSES, jnp.exp(logits), 0.0)
    total = jnp.sum(expon, axis=1, keepdims=True)
    each = jnp.log(total) - jnp.sum(logits * onehot, axis=1, keepdims=True)
    loss[...] = jnp.sum(each, axis=0, keepdims=True) * (1.0 / SEEDS)
    g3[...] = ((expon / total - onehot) * (1.0 / SEEDS)).astype(BF)

    sw_g3 = link(g3, rg3, sibling)
    keep3, keep2, give3, give2 = rest_keep
    give3[...] = jnp.where(k == 0, mean3[...], act2[0:SEEDS])
    keep3[...] = jnp.where(k == 0, act2[0:SEEDS], mean3[...])
    sw_a3 = link(give3, ra3, sibling)
    give2[...] = jnp.where(k == 0, mean2[...], act1[0:R2])
    keep2[...] = jnp.where(k == 0, act1[0:R2], mean2[...])
    sw_a2 = link(give2, ra2, sibling)
    for n in range(4):
        back = (dot(g3[...], top[1, :, lanes(n)]) * (1.0 / FAN3)).astype(BF)
        own = dot(g3[...], top[0, :, lanes(n)])
        grad = dot(counts3t[:R2, :SEEDS], back) + jnp.concatenate([own, jnp.zeros((R2 - SEEDS, 256), F32)], axis=0)
        g2[:, lanes(n)] = (grad * slope(pre2[:, lanes(n)])).astype(BF)
    sw_g2 = link(g2, rg2, sibling)

    class Ring:
        def __init__(self, block, add, up, down, relay, direct, comb):
            self.block, self.add, self.up, self.down = block, add, up, down
            self.relay, self.direct, self.comb = relay, direct, comb

        def opposite(self):
            self.n_relay = (
                link(self.block(2, 0), self.relay.at[0], self.up), link(self.block(2, 1), self.relay.at[1], self.down)
            )

        def to_up(self):
            self.n_up = link(self.block(1, 1), self.direct.at[1], self.up)

        def to_down(self):
            self.n_down = link(self.block(3, 0), self.direct.at[0], self.down)

        def pass_on(self):
            self.n_comb = []
            for h, off, to in ((0, 1, self.up), (1, 3, self.down)):
                arrived(self.n_relay[h], self.relay.at[h])
                self.add(self.relay.at[h], (self.relay.at[h], self.block(off, h)))
                self.n_comb.append(link(self.relay.at[h], self.comb.at[h], to))

        def finish(self, out):
            for h, n in ((0, self.n_down), (1, self.n_up)):
                arrived(self.n_comb[h], self.comb.at[h])
                arrived(n, self.direct.at[h])
                self.add(out(h), (self.block(0, h), self.comb.at[h], self.direct.at[h]))

    def add_leading(dst, parts):
        def body(i, _):
            v = parts[0][i].astype(F32)
            for p in parts[1:]:
                v = v + p[i].astype(F32)
            dst[i] = v.astype(BF)
            return 0

        lax.fori_loop(0, dst.shape[0], body, 0)

    class Chunk:
        def __init__(self, sizes, bufs, out):
            self.rows, self.out = sizes, out
            (
                self.s1, self.s2, rel1, dir1, com1, rel2, dir2, com2, self.t1, self.t2, self.q1, self.q2, self.u,
            ) = bufs[:13]
            self.y = Ring(
                lambda off, h: self.s1.at[ys[off], pl.ds(8 * h, 8)], add_leading, peer(dy=1), peer(dy=3), rel1, dir1, com1
            )
            self.x = Ring(
                lambda off, h: self.s2.at[:, pl.ds(xs[off] * 4 + 2 * h, 2)],
                add_leading, peer(dx=1), peer(dx=3), rel2, dir2, com2,
            )

        def first_y_done(self):
            self.y.finish(lambda h: self.t1.at[pl.ds(8 * h, 8)])
            self.n1 = [link(self.t1.at[mine_x(s)], self.q1.at[s - 1], peer(dx=s)) for s in range(1, 4)]

        def first_x_done(self):
            self.x.finish(lambda h: self.t2.at[:, pl.ds(2 * h, 2)])
            self.n2 = [link(self.t2.at[ys[s]], self.q2.at[s - 1], peer(dy=s)) for s in range(1, 4)]

        def second_done(self, rz):
            r1, r2 = self.rows
            for lo, hi, numbers, t, q in (
                (0, r1, self.n1, lambda h: self.t1[x * 4 + h], self.q1),
                (r1, r1 + r2, self.n2, lambda h: self.t2[y, h], self.q2),
            ):
                for s in range(3):
                    arrived(numbers[s], q.at[s])
                for h in range(4):
                    v = t(h).astype(F32)
                    for s in range(3):
                        v = v + q[s, h].astype(F32)
                    v = v.astype(BF)
                    self.u[0, h, lo:hi] = v[:, 0:128]
                    self.u[1, h, lo:hi] = v[:, 128:256]
            self.rz = rz
            self.n3 = []
            for s in range(1, 8):
                p = (zl * 4 + zh + s) % 8
                self.n3.append(link(self.u.at[p // 4, p % 4], rz.at[s - 1], device(x, y, p % 4, p // 4, k)))

        def third_done(self):
            v = self.u[zl, zh].astype(F32)
            for s in range(7):
                arrived(self.n3[s], self.rz.at[s])
                v = v + self.rz[s].astype(F32)
            self.mine = y * 2 + zl
            piece = self.out.at[k, self.mine]
            self.out[k, self.mine] = v.astype(BF)
            self.n4 = []
            for s in range(1, 8):
                p = (self.mine + s) % 8
                self.n4.append(link(piece, piece, device(x, p // 2, zh, p % 2, k)))
            self.n5 = [link(piece, piece, sibling)]

        def gathered(self):
            for s in range(1, 8):
                piece = self.out.at[k, (self.mine + 8 - s) % 8]
                arrived(self.n4[s - 1], piece)
                self.n5.append(link(piece, piece, sibling))

        def done(self):
            for s in range(8):
                arrived(self.n5[s], self.out.at[1 - k, (self.mine + 8 - s) % 8])

    upper, lower = Chunk(UPPER, bufs_a, out_a), Chunk(LOWER, bufs_b, out_b)
    order = (2, 1, 3, 0)

    arrived(sw_g3, rg3)
    arrived(sw_a3, ra3)
    third = (dot(keep3[...].T, g3[...]) + dot(ra3[...].T, rg3[...])).astype(BF).reshape(CUTS, 4, 16, 256)
    for j in range(4):
        upper.s2[j, :, 16:32] = third[:, j]
    keep_t = keep2[...].T
    arrived(sw_a2, ra2)
    sib_t = ra2[...].T
    arrived(sw_g2, rg2)
    for off in order:
        n = ys[off]
        p = (dot(keep_t, g2[:, lanes(n)]) + dot(sib_t, rg2[:, lanes(n)])).astype(BF).reshape(CUTS, 64, 256)
        upper.s1[n] = p[:, 0:48]
        upper.s2[n, :, 0:16] = p[:, 48:64]
        if off == 2:
            upper.y.opposite()
        if off == 1:
            upper.y.to_up()
        if off == 3:
            upper.y.to_down()
    upper.x.opposite()
    upper.x.to_up()
    upper.x.to_down()

    for n in range(4):
        back2[0:R2, lanes(n)] = (dot_nt(g2[...], second[1, lanes(n), :]) * (1.0 / FAN2)).astype(BF)
    for n in range(4):
        own = dot_nt(g2[...], second[0, lanes(n), :])
        grad = dot(counts2t[:R1], back2[:, lanes(n)]) + jnp.concatenate(
            [own, jnp.zeros((R1 - R2, 256), F32)], axis=0
        )
        g1[:, lanes(n)] = (grad * slope(pre1[:, lanes(n)])).astype(BF)
    sw_g1 = link(g1, rg1, sibling)
    upper.y.pass_on()
    arrived(sw_a1, ra1)
    arrived(sw_g1, rg1)
    for off in order:
        n = ys[off]
        p = (dot(at[k], g1[:, lanes(n)]) + dot(ra1[...], rg1[:, lanes(n)])).astype(BF).reshape(CUTS, 48, 256)
        lower.s1[n] = p[:, 0:16]
        lower.s2[n] = p[:, 16:48]
        if off == 2:
            lower.y.opposite()
        if off == 1:
            lower.y.to_up()
            upper.x.pass_on()
        if off == 3:
            lower.y.to_down()
    lower.x.opposite()
    lower.x.to_up()
    lower.x.to_down()
    upper.first_y_done()
    lower.y.pass_on()
    upper.first_x_done()
    lower.x.pass_on()
    upper.second_done(rest_rz[0])
    lower.first_y_done()
    lower.first_x_done()
    upper.third_done()
    lower.second_done(rest_rz[1])
    upper.gathered()
    lower.third_done()
    lower.gathered()
    upper.done()
    lower.done()

    for cp in sends:
        cp.wait_send()

    def sent(s, _):
        a_copy(s).wait_send()
        return 0

    lax.fori_loop(1, CUTS, sent, 0)


def step(*operands):
    dma = pltpu.SemaphoreType.DMA
    vm = lambda *shape: pltpu.VMEM(shape, BF)
    vf = lambda *shape: pltpu.VMEM(shape, F32)
    vi = lambda *shape: pltpu.VMEM(shape, jnp.int32)

    def chunk(sizes):
        r1, r2 = sizes
        return [
            vm(4, CUTS, r1, 256), vm(4, CUTS, r2, 256),
            vm(2, 8, r1, 256), vm(2, 8, r1, 256), vm(2, 8, r1, 256),
            vm(2, 4, 2, r2, 256), vm(2, 4, 2, r2, 256), vm(2, 4, 2, r2, 256),
            vm(CUTS, r1, 256), vm(4, 4, r2, 256),
            vm(3, 4, r1, 256), vm(3, 4, r2, 256),
            vm(2, 4, r1 + r2, 128),
        ]

    return pl.pallas_call(
        kernel,
        out_shape=(
            jax.ShapeDtypeStruct((1, 1), F32),
            jax.ShapeDtypeStruct((2, 8, sum(UPPER), 128), BF),
            jax.ShapeDtypeStruct((2, 8, sum(LOWER), 128), BF),
        ),
        in_specs=[ANY] * 11,
        out_specs=(VMEM,) * 3,
        scratch_shapes=[
            vi(FAN1, CUTS, R1), vi(FAN2, 1, R2), vi(FAN3, 1, SEEDS), vi(1, SEEDS), vi(16, 256), vm(CUTS, WIDE, R0), vm(2, WIDE, HID), vm(2, HID, HID),
            vm(2, CLASSES, HID), vm(2, PADDED, HID),
            vm(CUTS, 144, 128), vm(CUTS, 144, 128), vm(2, CUTS, WIDE, 512), vm(2, 4, CUTS, WIDE, 128), vm(2, ROWS, R1),
            vf(R1, HID), vm(256, HID), vm(R2, HID), vf(R2, HID), vm(256, HID), vm(SEEDS, HID), vm(256, HID),
            vm(R1, HID), vm(R2, HID), vm(SEEDS, PADDED),
            vm(ROWS, R1), vm(R2, HID), vm(SEEDS, HID), vm(R1, HID), vm(R2, HID), vm(SEEDS, PADDED),
        ]
        + chunk(UPPER)
        + chunk(LOWER)
        + [
            vm(SEEDS, HID), vm(R2, HID), vm(SEEDS, HID), vm(R2, HID),
            vm(7, sum(UPPER), 128), vm(7, sum(LOWER), 128),
            dma((40,)), dma((SLOTS,)), dma((SLOTS,)), dma((15,)), dma((15,)),
        ],
        compiler_params=pltpu.CompilerParams(
            collective_id=1, has_side_effects=True, vmem_limit_bytes=56 * 2**20
        ),
    )(*operands)


def finish_kernel(upper, lower, first_self, first_neigh, second_self, second_neigh, third_self, third_neigh):
    for k, first, second, third in (
        (0, first_self, second_self, third_self), (1, first_neigh, second_neigh, third_neigh)
    ):
        for g in range(8):
            first[:, lanes(g, 128)] = lower[k, g].astype(F32)
            second[:, lanes(g, 128)] = upper[k, g, 0:64].astype(F32)
            lo = (g % 2) * 128
            width = min(128, CLASSES - lo)
            third[g // 2 * 16:g // 2 * 16 + 16, lo:lo + width] = upper[k, g, 64:80, 0:width].astype(F32)


def finish(upper, lower):
    shapes = ((48, HID), (48, HID), (64, HID), (64, HID), (64, CLASSES), (64, CLASSES))
    return pl.pallas_call(
        finish_kernel,
        out_shape=tuple(jax.ShapeDtypeStruct(s, F32) for s in shapes),
        in_specs=[VMEM] * 2,
        out_specs=(VMEM,) * 6,
    )(upper, lower)


def per_device(
    features, lists_one, lists_two, lists_three, labels, initial_node_weight, initial_neighbour_weight,
    second_self, second_neigh, final_node_weight, third_neigh,
):
    xt = jnp.swapaxes(features[0], 1, 2)
    lists = jnp.transpose(lists_one[0], (2, 0, 1))

    loss, upper, lower = step(
        lists, xt, initial_node_weight, initial_neighbour_weight, second_self, second_neigh,
        final_node_weight.T, third_neigh.T,
        jnp.transpose(lists_two[0], (2, 0, 1)), jnp.transpose(lists_three[0], (2, 0, 1)), labels[0],
    )
    return (loss,) + tuple(finish(upper, lower))


def solution(mesh):
    return jax.shard_map(
        per_device,
        mesh=mesh,
        in_specs=(
            P("dp", None, None, "cuts"),
            P("dp", None, None, None),
            P("dp", "cuts", None, None),
            P("dp", "cuts", None, None),
            P("dp", "cuts", None),
            P("cuts", None),
            P("cuts", None),
            P(), P(), P(), P(),
        ),
        out_specs=(P("dp", "cuts"),) + (P("cuts", None),) * 6,
        check_vma=False,
    )
```

```python
import jax
import jax.numpy as jnp
from jax import lax
from jax.experimental import pallas as pl
from jax.experimental.pallas import tpu as pltpu
from jax.sharding import PartitionSpec as P

MESH = pl.DeviceIdType.MESH
BF = jnp.bfloat16
F32 = jnp.float32
FAN1 = 5
FAN2 = 5
FAN3 = 3
R0 = 1024
R1 = 192
R2 = 160
SEEDS = 128
HID = 1024
CUTS = 16
WIDE = 48
ROWS = CUTS * WIDE
CLASSES = 153
PADDED = 256
VMEM = pl.BlockSpec(memory_space=pltpu.VMEM)
ANY = pl.BlockSpec(memory_space=pl.ANY)
SLOTS = 80
UPPER = (32, 32, 16)
LOWER = (16, 16, 16)


def dot(a, b):
    return jnp.dot(a, b, preferred_element_type=F32)


def dot_nt(a, b):
    return lax.dot_general(a, b, (((1,), (1,)), ((), ())), preferred_element_type=F32)


def sigmoid(v):
    return 1.0 / (1.0 + jnp.exp(-v))


def slope(v):
    s = sigmoid(v)
    return s * (1.0 + v * (1.0 - s))


def lanes(n, width=256):
    if isinstance(n, int):
        return slice(n * width, (n + 1) * width)
    return pl.ds(pl.multiple_of(n * width, width), width)


def kernel(
    lists_hbm, xt_hbm, w_self_hbm, w_neigh_hbm, second_self_hbm, second_neigh_hbm, final_hbm, third_hbm,
    lists2_hbm, lists3_hbm, labels_hbm,
    loss, out_a, out_b,
    lists, lists2, lists3, labels, idx, xt, w_in, second, raw, top,
    blk_out, blk_in, wa, wb, at,
    pre1, act1, mean2, pre2, act2, mean3, back2, g1, g2, g3,
    ra1, ra2, ra3, rg1, rg2, rg3,
    *rest,
):
    bufs_a, bufs_b = rest[:17], rest[17:34]
    rest_keep, rest_rz = rest[34:38], rest[38:42]
    load, send, recv, a_send, a_recv = rest[42:]
    d, c = lax.axis_index("dp"), lax.axis_index("cuts")
    x, y, zh, zl, k = c // 4, d // 4, c % 4, (d // 2) % 2, d % 2
    me = c

    def device(px, py, pzh, pzl, pk):
        return {"dp": (py * 2 + pzl) * 2 + pk, "cuts": px * 4 + pzh}

    def peer(dx=0, dy=0, dzh=0, dzl=0, dk=0):
        return device((x + dx) % 4, (y + dy) % 4, (zh + dzh) % 4, (zl + dzl) % 2, (k + dk) % 2)

    sibling = peer(dk=1)
    xs = [(x + s) % 4 for s in range(4)]
    quads = [pl.ds(pl.multiple_of(v * 4, 4), 4) for v in xs]
    behinds = [x * 4 + (zh + 4 - j) % 4 for j in range(4)]
    ys = [(y + s) % 4 for s in range(4)]

    barrier = pltpu.get_barrier_semaphore()
    peers = [peer(dx=s // 4, dzh=s % 4) for s in range(1, 16)]
    peers += [peer(dy=s // 2, dzl=s % 2) for s in range(1, 8)]
    peers += [peer(dzh=s, dzl=1) for s in range(1, 4)]
    peers += [peer(dx=i, dy=j) for i in range(1, 4) for j in range(1, 4)]
    peers += [sibling]
    for p in peers:
        pl.semaphore_signal(barrier, 1, device_id=p, device_id_type=MESH)

    count = [0]

    def fetch(src, dst):
        cp = pltpu.make_async_copy(src, dst, load.at[count[0]])
        count[0] += 1
        cp.start()
        return cp

    ld_lists = fetch(lists_hbm, lists)
    ld_idx = [fetch(lists2_hbm, lists2), fetch(lists3_hbm, lists3), fetch(labels_hbm, labels)]
    ld_w = [fetch(w_self_hbm, w_in.at[0]), fetch(w_neigh_hbm, w_in.at[1])]

    def xt_copy(s):
        m = (me + s) % CUTS
        return pltpu.make_async_copy(xt_hbm.at[m], xt.at[m], load.at[16 + s])

    def xt_start(s, _):
        xt_copy(s).start()
        return 0

    lax.fori_loop(1, CUTS + 1, xt_start, 0)
    ld_top = [fetch(final_hbm, raw.at[0]), fetch(third_hbm, raw.at[1])]
    ld_second = [fetch(second_self_hbm, second.at[0]), fetch(second_neigh_hbm, second.at[1])]

    sends = []

    def start(n, src, dst, to):
        pltpu.make_async_remote_copy(
            src_ref=src, dst_ref=dst, send_sem=send.at[n], recv_sem=recv.at[n], device_id=to, device_id_type=MESH
        ).start()

    def link_all(whole, copies):
        n = len(sends)
        sends.append(whole)
        for src, dst, to in copies:
            start(n, src, dst, to)
        return n

    def link(src, dst, to):
        return link_all(src, [(src, dst, to)])

    def pair_of(n, ref):
        return pltpu.make_async_remote_copy(
            src_ref=ref, dst_ref=ref, send_sem=send.at[n], recv_sem=recv.at[n], device_id=sibling, device_id_type=MESH
        )

    def arrived(n, dst):
        pair_of(n, dst).wait_recv()

    for cp in ld_w:
        cp.wait()
    wa[k, me] = w_in[k, :, 0:512]
    wb[k, y, me] = w_in[k, :, pl.ds(pl.multiple_of(512 + y * 128, 128), 128)]
    ld_lists.wait()
    pl.semaphore_wait(barrier, len(peers))

    wbz = [link(wb.at[k, y, me], wb.at[k, y, me], peer(dzh=s)) for s in range(1, 4)]
    def across(j):
        src = wa.at[k, behinds[j]]
        for s in range(1, 4):
            start(wax[s - 1], src, src, peer(dx=s))

    wax = [link_all(wa.at[k, quads[0]], []) for s in range(1, 4)]
    waz = [link(wa.at[k, me], wa.at[k, me], peer(dzh=s)) for s in range(1, 4)]

    across(0)

    def block(m):
        one, zero = jnp.ones((16, R1), BF), jnp.zeros((16, R1), BF)
        wanted = [jnp.broadcast_to(lists[f, pl.ds(m, 1), :], (16, R1)).astype(jnp.int16) for f in range(FAN1)]
        base = lax.broadcasted_iota(jnp.int32, (16, R1), 0).astype(jnp.int16)
        parts = []
        for b in range(R0 // 16):
            row = base + jnp.int16(16 * b)
            v = jnp.where(row == wanted[0], one, zero)
            for f in range(1, FAN1):
                v = v + jnp.where(row == wanted[f], one, zero)
            parts.append(v)
        mean = (dot(xt[m], jnp.concatenate(parts, axis=0)) * (1.0 / FAN1)).astype(BF)
        return xt[m][:, :R1], mean

    def pack(ref, m, own, mean):
        ref[m, 0:48] = own[:, 0:128]
        ref[m, 48:96] = mean[:, 0:128]
        ref[m, 96:144] = jnp.concatenate([own[:, 128:192], mean[:, 128:192]], axis=1)

    def a_pair(s=None):
        here = pl.ds(0, CUTS - 1) if s is None else s - 1
        return pltpu.make_async_remote_copy(
            src_ref=blk_out.at[here], dst_ref=blk_in.at[here], send_sem=a_send.at[0], recv_sem=a_recv.at[0],
            device_id=sibling if s is None else {"dp": d, "cuts": (me + s) % CUTS}, device_id_type=MESH,
        )

    def one(s, _):
        xt_copy(s).wait()
        own, mean = block((me + s) % CUTS)
        pack(blk_out, s - 1, own, mean)

        @pl.when(s < CUTS)
        def _():
            a_pair(s).start()

        @pl.when(s == 6)
        def _():
            for j in range(1, 4):
                arrived(wbz[j - 1], wb.at[k, y, behinds[j]])
            for s in range(1, 4):
                wbx.append(link(wb.at[k, y, quads[0]], wb.at[k, y, quads[0]], peer(dx=s)))

        @pl.when(s == 8)
        def _():
            for j in (1, 3):
                arrived(waz[j - 1], wa.at[k, behinds[j]])
                across(j)

        @pl.when(s == 11)
        def _():
            for s in range(1, 4):
                arrived(wbx[s - 1], wb.at[k, y, quads[-s]])
            for s in range(1, 4):
                wby.append(link(wb.at[k, y], wb.at[k, y], peer(dy=s)))
            wbk.append(link(wb.at[k, y], wb.at[k, y], sibling))

        @pl.when(s == 13)
        def _():
            arrived(waz[1], wa.at[k, behinds[2]])
            across(2)
            wak.append(link(wa.at[k, quads[0]], wa.at[k, quads[0]], sibling))

        return 0

    wbx, wby, wak, wbk = [], [], [], []
    lax.fori_loop(1, CUTS + 1, one, 0)

    for cp in ld_top:
        cp.wait()
    for i in range(2):
        top[i, 144:256] = jnp.zeros((112, HID), BF)
        top[i, 0:CLASSES] = raw[i]
    for cp in ld_idx:
        cp.wait()
    idx[...] = jnp.full((16, 256), -1, jnp.int32)
    for f in range(FAN2):
        idx[f:f + 1, 0:R2] = lists2[f]
    for f in range(FAN3):
        idx[FAN2 + f:FAN2 + f + 1, 0:SEEDS] = lists3[f]
    idx[8:9, 0:SEEDS] = labels[...]
    rows256 = lax.broadcasted_iota(jnp.int32, (256, 256), 0)

    def counting(first, fan):
        counts = jnp.zeros((256, 256), F32)
        for f in range(first, first + fan):
            counts = counts + jnp.where(rows256 == idx[f:f + 1, :], 1.0, 0.0)
        return counts

    counts2t, counts3t = counting(0, FAN2), counting(FAN2, FAN3)
    counts2, counts3 = counts2t.T.astype(BF), counts3t.T.astype(BF)
    counts2t, counts3t = counts2t.astype(BF), counts3t.astype(BF)
    onehot = jnp.where(rows256 == idx[8:9, :], 1.0, 0.0).T[:SEEDS]
    act1[R1:256] = jnp.zeros((256 - R1, HID), BF)
    act2[R2:256] = jnp.zeros((256 - R2, HID), BF)
    back2[R2:256] = jnp.zeros((256 - R2, HID), BF)

    for s in range(1, 4):
        arrived(wax[s - 1], wa.at[k, quads[-s]])
        wak.append(link(wa.at[k, quads[-s]], wa.at[k, quads[-s]], sibling))
    a_pair().wait_recv()
    for s in range(CUTS):
        src, ref, i = (me + CUTS - s) % CUTS, blk_in if s else blk_out, s - 1 if s else CUTS - 1
        here = pl.ds(pl.multiple_of(src * WIDE, WIDE), WIDE)
        tail = ref[i, 96:144]
        at[0, here, 0:128] = ref[i, 0:48]
        at[1, here, 0:128] = ref[i, 48:96]
        at[0, here, 128:192] = tail[:, 0:64]
        at[1, here, 128:192] = tail[:, 64:128]
    sw_a1 = link(at.at[1 - k], ra1, sibling)
    at0, at1 = at[0].T, at[1].T
    for s in range(1, 4):
        frm = (y + 4 - s) % 4
        arrived(wby[s - 1], wb.at[k, frm])
        wbk.append(link(wb.at[k, frm], wb.at[k, frm], sibling))

    for n in range(4):
        if n == 0:
            for s in range(4):
                arrived(wak[s], wa.at[1 - k, quads[-s]])
        if n == 2:
            for s in range(4):
                arrived(wbk[s], wb.at[1 - k, (y + 4 - s) % 4])
        if n < 2:
            w0, w1 = (wa[i, :, :, lanes(n)].reshape(ROWS, 256) for i in range(2))
        else:
            q = 2 * n - 4
            w0, w1 = (
                jnp.concatenate([wb[i, q].reshape(ROWS, 128), wb[i, q + 1].reshape(ROWS, 128)], axis=1)
                for i in range(2)
            )
        v = dot(at0, w0) + dot(at1, w1)
        pre1[:, lanes(n)] = v
        act1[0:R1, lanes(n)] = (v * sigmoid(v)).astype(BF)
    for n in range(4):
        mean2[:, lanes(n)] = (dot(counts2[:R2], act1[:, lanes(n)]) * (1.0 / FAN2)).astype(BF)
    for cp in ld_second:
        cp.wait()
    for n in range(4):
        v = dot(act1[0:R2], second[0, :, lanes(n)]) + dot(mean2[...], second[1, :, lanes(n)])
        pre2[:, lanes(n)] = v
        act2[0:R2, lanes(n)] = (v * sigmoid(v)).astype(BF)
    for n in range(4):
        mean3[:, lanes(n)] = (dot(counts3[:SEEDS], act2[:, lanes(n)]) * (1.0 / FAN3)).astype(BF)
    logits = dot_nt(act2[0:SEEDS], top[0]) + dot_nt(mean3[...], top[1])
    column = lax.broadcasted_iota(jnp.int32, (SEEDS, PADDED), 1)
    expon = jnp.where(column < CLASSES, jnp.exp(logits), 0.0)
    total = jnp.sum(expon, axis=1, keepdims=True)
    each = jnp.log(total) - jnp.sum(logits * onehot, axis=1, keepdims=True)
    loss[...] = jnp.sum(each, axis=0, keepdims=True) * (1.0 / SEEDS)
    g3[...] = ((expon / total - onehot) * (1.0 / SEEDS)).astype(BF)

    sw_g3 = link(g3, rg3, sibling)
    keep3, keep2, give3, give2 = rest_keep
    give3[...] = jnp.where(k == 0, mean3[...], act2[0:SEEDS])
    keep3[...] = jnp.where(k == 0, act2[0:SEEDS], mean3[...])
    sw_a3 = link(give3, ra3, sibling)
    give2[...] = jnp.where(k == 0, mean2[...], act1[0:R2])
    keep2[...] = jnp.where(k == 0, act1[0:R2], mean2[...])
    sw_a2 = link(give2, ra2, sibling)
    for n in range(4):
        back = (dot(g3[...], top[1, :, lanes(n)]) * (1.0 / FAN3)).astype(BF)
        own = dot(g3[...], top[0, :, lanes(n)])
        grad = dot(counts3t[:R2, :SEEDS], back) + jnp.concatenate([own, jnp.zeros((R2 - SEEDS, 256), F32)], axis=0)
        g2[:, lanes(n)] = (grad * slope(pre2[:, lanes(n)])).astype(BF)
    sw_g2 = link(g2, rg2, sibling)

    class Ring:
        def __init__(self, block, add, up, down, relay, direct, comb):
            self.block, self.add, self.up, self.down = block, add, up, down
            self.relay, self.direct, self.comb = relay, direct, comb

        def opposite(self):
            self.n_relay = (
                link(self.block(2, 0), self.relay.at[0], self.up), link(self.block(2, 1), self.relay.at[1], self.down)
            )

        def to_up(self):
            self.n_up = link(self.block(1, 1), self.direct.at[1], self.up)

        def to_down(self):
            self.n_down = link(self.block(3, 0), self.direct.at[0], self.down)

        def pass_on(self):
            self.n_comb = []
            for h, off, to in ((0, 1, self.up), (1, 3, self.down)):
                arrived(self.n_relay[h], self.relay.at[h])
                self.add(self.relay.at[h], (self.relay.at[h], self.block(off, h)))
                self.n_comb.append(link(self.relay.at[h], self.comb.at[h], to))

        def finish(self, out):
            for h, n in ((0, self.n_down), (1, self.n_up)):
                arrived(self.n_comb[h], self.comb.at[h])
                arrived(n, self.direct.at[h])
                self.add(out(h), (self.block(0, h), self.comb.at[h], self.direct.at[h]))

    def add_leading(dst, parts):
        def body(i, _):
            v = parts[0][i].astype(F32)
            for p in parts[1:]:
                v = v + p[i].astype(F32)
            dst[i] = v.astype(BF)
            return 0

        lax.fori_loop(0, dst.shape[0], body, 0)

    class Chunk:
        def __init__(self, sizes, bufs, out, back):
            self.rows, self.out, self.back = sizes, out, back
            (
                self.s1, self.s2, rel1, dir1, com1, rel2, dir2, com2, self.t1, self.t2, self.q1, self.q2, self.u,
                self.sz, self.rz1, self.tz, self.rt,
            ) = bufs
            self.y = Ring(
                lambda off, h: self.s1.at[ys[off], pl.ds(8 * h, 8)], add_leading, peer(dy=1), peer(dy=3), rel1, dir1, com1
            )
            self.x = Ring(
                lambda off, h: self.s2.at[:, pl.ds(xs[off] * 4 + 2 * h, 2)],
                add_leading, peer(dx=1), peer(dx=3), rel2, dir2, com2,
            )

        def first_y_done(self):
            self.y.finish(lambda h: self.t1.at[pl.ds(8 * h, 8)])
            self.n1 = link_all(self.q1, [(self.t1.at[quads[s]], self.q1.at[s - 1], peer(dx=s)) for s in range(1, 4)])

        def first_x_done(self):
            self.x.finish(lambda h: self.t2.at[:, pl.ds(2 * h, 2)])
            self.n2 = link_all(self.q2, [(self.t2.at[ys[s]], self.q2.at[s - 1], peer(dy=s)) for s in range(1, 4)])

        def fill_z(self, n, v):
            for i in range(CUTS):
                for h in range(2):
                    self.sz[h, i % 4, i // 4, n] = v[i, :, lanes(h, 128)]

        def z_first(self):
            far = [(zl * 4 + zh + s) % 8 for s in range(1, 8)]
            self.n6 = link_all(
                self.rz1,
                [(self.sz.at[p // 4, p % 4], self.rz1.at[s], device(x, y, p % 4, p // 4, k)) for s, p in enumerate(far)],
            )

        def z_sum(self):
            arrived(self.n6, self.rz1)
            for i in range(4):
                v = self.sz[zl, zh, i].astype(F32)
                for s in range(7):
                    v = v + self.rz1[s, i].astype(F32)
                self.tz[i] = v.astype(BF)
            self.n7 = link_all(
                self.rt,
                [
                    (self.tz.at[xs[q // 4], ys[q % 4]], self.rt.at[q - 1], peer(dx=q // 4, dy=q % 4))
                    for q in range(1, 16)
                ],
            )

        def second_done(self, rz):
            r1, r2, _ = self.rows
            for lo, hi, number, t, q in (
                (0, r1, self.n1, lambda h: self.t1[x * 4 + h], self.q1),
                (r1, r1 + r2, self.n2, lambda h: self.t2[y, h], self.q2),
            ):
                arrived(number, q)
                for h in range(4):
                    v = t(h).astype(F32)
                    for s in range(3):
                        v = v + q[s, h].astype(F32)
                    v = v.astype(BF)
                    self.u[0, h, lo:hi] = v[:, 0:128]
                    self.u[1, h, lo:hi] = v[:, 128:256]
            self.rz = rz
            far = [(zl * 4 + zh + s) % 8 for s in range(1, 8)]
            self.n3 = link_all(
                rz, [(self.u.at[p // 4, p % 4], rz.at[s], device(x, y, p % 4, p // 4, k)) for s, p in enumerate(far)]
            )

        def third_done(self):
            v = self.u[zl, zh].astype(F32)
            arrived(self.n3, self.rz)
            for s in range(7):
                v = v + self.rz[s].astype(F32)
            self.mine = y * 2 + zl
            piece = self.out.at[k, self.mine]
            rows = self.rows[0] + self.rows[1]
            self.out[k, self.mine, 0:rows] = v.astype(BF)
            arrived(self.n7, self.rt)
            v = self.tz[x, y].astype(F32)
            for s in range(15):
                v = v + self.rt[s].astype(F32)
            self.out[k, self.mine, rows:rows + 16] = v.astype(BF)
            far = [(self.mine + s) % 8 for s in range(1, 8)]
            self.n4 = link_all(
                self.back, [(piece, self.back.at[s], device(x, p // 2, zh, p % 2, k)) for s, p in enumerate(far)]
            )

        def gathered(self):
            arrived(self.n4, self.back)
            for s in range(1, 8):
                self.out[k, (self.mine + 8 - s) % 8] = self.back[s - 1]
            self.n5 = link(self.out.at[k], self.out.at[k], sibling)

        def done(self):
            arrived(self.n5, self.out.at[1 - k])

    upper, lower = Chunk(UPPER, bufs_a, out_a, rest_rz[2]), Chunk(LOWER, bufs_b, out_b, rest_rz[3])
    order = (2, 1, 3, 0)

    arrived(sw_g3, rg3)
    arrived(sw_a3, ra3)
    third = (dot(keep3[...].T, g3[...]) + dot(ra3[...].T, rg3[...])).astype(BF).reshape(CUTS, 4, 16, 256)
    for j in range(4):
        upper.fill_z(j, third[:, j])
    upper.z_first()
    keep_t = keep2[...].T
    arrived(sw_a2, ra2)
    sib_t = ra2[...].T
    arrived(sw_g2, rg2)
    for off in order:
        n = ys[off]
        p = (dot(keep_t, g2[:, lanes(n)]) + dot(sib_t, rg2[:, lanes(n)])).astype(BF).reshape(CUTS, 64, 256)
        upper.s1[n] = p[:, 0:32]
        upper.s2[n] = p[:, 32:64]
        if off == 2:
            upper.y.opposite()
        if off == 1:
            upper.y.to_up()
        if off == 3:
            upper.y.to_down()
    upper.x.opposite()
    upper.x.to_up()
    upper.x.to_down()

    for n in range(4):
        back2[0:R2, lanes(n)] = (dot_nt(g2[...], second[1, lanes(n), :]) * (1.0 / FAN2)).astype(BF)
    for n in range(4):
        own = dot_nt(g2[...], second[0, lanes(n), :])
        grad = dot(counts2t[:R1], back2[:, lanes(n)]) + jnp.concatenate(
            [own, jnp.zeros((R1 - R2, 256), F32)], axis=0
        )
        g1[:, lanes(n)] = (grad * slope(pre1[:, lanes(n)])).astype(BF)
    sw_g1 = link(g1, rg1, sibling)
    upper.y.pass_on()
    arrived(sw_a1, ra1)
    arrived(sw_g1, rg1)
    for off in order:
        n = ys[off]
        p = (dot(at[k], g1[:, lanes(n)]) + dot(ra1[...], rg1[:, lanes(n)])).astype(BF).reshape(CUTS, 48, 256)
        lower.s1[n] = p[:, 0:16]
        lower.s2[n] = p[:, 16:32]
        lower.fill_z(n, p[:, 32:48])
        if off == 2:
            lower.y.opposite()
        if off == 1:
            lower.y.to_up()
            upper.x.pass_on()
        if off == 3:
            lower.y.to_down()
    lower.z_first()
    lower.x.opposite()
    lower.x.to_up()
    lower.x.to_down()
    upper.first_y_done()
    upper.first_x_done()
    upper.z_sum()
    lower.y.pass_on()
    lower.x.pass_on()
    upper.second_done(rest_rz[0])
    lower.first_y_done()
    lower.first_x_done()
    upper.third_done()
    lower.second_done(rest_rz[1])
    lower.z_sum()
    upper.gathered()
    lower.third_done()
    lower.gathered()
    upper.done()
    lower.done()

    for n, ref in enumerate(sends):
        pair_of(n, ref).wait_send()
    a_pair().wait_send()


def step(*operands):
    dma = pltpu.SemaphoreType.DMA
    vm = lambda *shape: pltpu.VMEM(shape, BF)
    vf = lambda *shape: pltpu.VMEM(shape, F32)
    vi = lambda *shape: pltpu.VMEM(shape, jnp.int32)

    def chunk(sizes):
        r1, r2, r3 = sizes
        return [
            vm(4, CUTS, r1, 256), vm(4, CUTS, r2, 256),
            vm(2, 8, r1, 256), vm(2, 8, r1, 256), vm(2, 8, r1, 256),
            vm(2, 4, 2, r2, 256), vm(2, 4, 2, r2, 256), vm(2, 4, 2, r2, 256),
            vm(CUTS, r1, 256), vm(4, 4, r2, 256),
            vm(3, 4, r1, 256), vm(3, 4, r2, 256),
            vm(2, 4, r1 + r2, 128),
            vm(2, 4, 4, 4, r3, 128), vm(7, 4, 4, r3, 128), vm(4, 4, r3, 128), vm(15, r3, 128),
        ]

    return pl.pallas_call(
        kernel,
        out_shape=(
            jax.ShapeDtypeStruct((1, 1), F32),
            jax.ShapeDtypeStruct((2, 8, sum(UPPER), 128), BF),
            jax.ShapeDtypeStruct((2, 8, sum(LOWER), 128), BF),
        ),
        in_specs=[ANY] * 11,
        out_specs=(VMEM,) * 3,
        scratch_shapes=[
            vi(FAN1, CUTS, R1), vi(FAN2, 1, R2), vi(FAN3, 1, SEEDS), vi(1, SEEDS), vi(16, 256), vm(CUTS, WIDE, R0), vm(2, WIDE, HID), vm(2, HID, HID),
            vm(2, CLASSES, HID), vm(2, PADDED, HID),
            vm(CUTS, 144, 128), vm(CUTS - 1, 144, 128), vm(2, CUTS, WIDE, 512), vm(2, 4, CUTS, WIDE, 128), vm(2, ROWS, R1),
            vf(R1, HID), vm(256, HID), vm(R2, HID), vf(R2, HID), vm(256, HID), vm(SEEDS, HID), vm(256, HID),
            vm(R1, HID), vm(R2, HID), vm(SEEDS, PADDED),
            vm(ROWS, R1), vm(R2, HID), vm(SEEDS, HID), vm(R1, HID), vm(R2, HID), vm(SEEDS, PADDED),
        ]
        + chunk(UPPER)
        + chunk(LOWER)
        + [
            vm(SEEDS, HID), vm(R2, HID), vm(SEEDS, HID), vm(R2, HID),
            vm(7, sum(UPPER[:2]), 128), vm(7, sum(LOWER[:2]), 128), vm(7, sum(UPPER), 128), vm(7, sum(LOWER), 128),
            dma((33,)), dma((SLOTS,)), dma((SLOTS,)), dma((1,)), dma((1,)),
        ],
        compiler_params=pltpu.CompilerParams(
            collective_id=1, has_side_effects=True, vmem_limit_bytes=56 * 2**20
        ),
    )(*operands)


def finish_kernel(upper, lower, first_self, first_neigh, second_self, second_neigh, third_self, third_neigh):
    for k, first, second, third in (
        (0, first_self, second_self, third_self), (1, first_neigh, second_neigh, third_neigh)
    ):
        for g in range(8):
            first[:, lanes(g, 128)] = lower[k, g].astype(F32)
            second[:, lanes(g, 128)] = upper[k, g, 0:64].astype(F32)
            lo = (g % 2) * 128
            width = min(128, CLASSES - lo)
            third[g // 2 * 16:g // 2 * 16 + 16, lo:lo + width] = upper[k, g, 64:80, 0:width].astype(F32)


def finish(upper, lower):
    shapes = ((48, HID), (48, HID), (64, HID), (64, HID), (64, CLASSES), (64, CLASSES))
    return pl.pallas_call(
        finish_kernel,
        out_shape=tuple(jax.ShapeDtypeStruct(s, F32) for s in shapes),
        in_specs=[VMEM] * 2,
        out_specs=(VMEM,) * 6,
    )(upper, lower)


def per_device(
    features, lists_one, lists_two, lists_three, labels, initial_node_weight, initial_neighbour_weight,
    second_self, second_neigh, final_node_weight, third_neigh,
):
    xt = jnp.swapaxes(features[0], 1, 2)
    lists = jnp.transpose(lists_one[0], (2, 0, 1))

    loss, upper, lower = step(
        lists, xt, initial_node_weight, initial_neighbour_weight, second_self, second_neigh,
        final_node_weight.T, third_neigh.T,
        jnp.transpose(lists_two[0], (2, 0, 1)), jnp.transpose(lists_three[0], (2, 0, 1)), labels[0],
    )
    return (loss,) + tuple(finish(upper, lower))


def solution(mesh):
    return jax.shard_map(
        per_device,
        mesh=mesh,
        in_specs=(
            P("dp", None, None, "cuts"),
            P("dp", None, None, None),
            P("dp", "cuts", None, None),
            P("dp", "cuts", None, None),
            P("dp", "cuts", None),
            P("cuts", None),
            P("cuts", None),
            P(), P(), P(), P(),
        ),
        out_specs=(P("dp", "cuts"),) + (P("cuts", None),) * 6,
        check_vma=False,
    )
```

```python
import jax
import jax.numpy as jnp
from jax import lax
from jax.experimental import pallas as pl
from jax.experimental.pallas import tpu as pltpu
from jax.sharding import PartitionSpec as P

MESH = pl.DeviceIdType.MESH
BF = jnp.bfloat16
F32 = jnp.float32
FAN1 = 5
FAN2 = 5
FAN3 = 3
R0 = 1024
R1 = 192
R2 = 160
SEEDS = 128
HID = 1024
CUTS = 16
WIDE = 48
ROWS = CUTS * WIDE
CLASSES = 153
PADDED = 256
VMEM = pl.BlockSpec(memory_space=pltpu.VMEM)
ANY = pl.BlockSpec(memory_space=pl.ANY)
SLOTS = 67
UPPER = (32, 32, 16)
LOWER = (16, 16, 16)


def dot(a, b):
    return jnp.dot(a, b, preferred_element_type=F32)


def dot_nt(a, b):
    return lax.dot_general(a, b, (((1,), (1,)), ((), ())), preferred_element_type=F32)


def sigmoid(v):
    return 1.0 / (1.0 + jnp.exp(-v))


def slope(v):
    s = sigmoid(v)
    return s * (1.0 + v * (1.0 - s))


def lanes(n, width=256):
    if isinstance(n, int):
        return slice(n * width, (n + 1) * width)
    return pl.ds(pl.multiple_of(n * width, width), width)


def kernel(
    lists_hbm, xt_hbm, w_self_hbm, w_neigh_hbm, second_self_hbm, second_neigh_hbm, final_hbm, third_hbm,
    lists2_hbm, lists3_hbm, labels_hbm,
    loss, out_a, out_b,
    lists, lists2, lists3, labels, idx, xt, w_in, second, raw, top,
    blk_out, blk_in, wa, wb, at,
    pre1, act1, mean2, pre2, act2, mean3, back2, g1, g2, g3,
    ra1, ra2, ra3, rg1, rg2, rg3,
    *rest,
):
    bufs_a, bufs_b = rest[:17], rest[17:34]
    rest_keep, rest_rz = rest[34:38], rest[38:42]
    load, send, recv, a_send, a_recv = rest[42:]
    d, c = lax.axis_index("dp"), lax.axis_index("cuts")
    x, y, zh, zl, k = c // 4, d // 4, c % 4, (d // 2) % 2, d % 2
    me = c

    def device(px, py, pzh, pzl, pk):
        return {"dp": (py * 2 + pzl) * 2 + pk, "cuts": px * 4 + pzh}

    def peer(dx=0, dy=0, dzh=0, dzl=0, dk=0):
        return device((x + dx) % 4, (y + dy) % 4, (zh + dzh) % 4, (zl + dzl) % 2, (k + dk) % 2)

    sibling = peer(dk=1)
    xs = [(x + s) % 4 for s in range(4)]
    quads = [pl.ds(pl.multiple_of(v * 4, 4), 4) for v in xs]
    behinds = [x * 4 + (zh + 4 - j) % 4 for j in range(4)]
    ys = [(y + s) % 4 for s in range(4)]

    barrier = pltpu.get_barrier_semaphore()
    peers = [peer(dx=s // 4, dzh=s % 4) for s in range(1, 16)]
    peers += [peer(dy=s // 2, dzl=s % 2) for s in range(1, 8)]
    peers += [peer(dzh=s, dzl=1) for s in range(1, 4)]
    peers += [peer(dx=i, dy=j) for i in range(1, 4) for j in range(1, 4)]
    peers += [sibling]
    for p in peers:
        pl.semaphore_signal(barrier, 1, device_id=p, device_id_type=MESH)

    count = [0]

    def fetch(src, dst):
        cp = pltpu.make_async_copy(src, dst, load.at[count[0]])
        count[0] += 1
        cp.start()
        return cp

    ld_lists = fetch(lists_hbm, lists)
    ld_idx = [fetch(lists2_hbm, lists2), fetch(lists3_hbm, lists3), fetch(labels_hbm, labels)]
    ld_w = [fetch(w_self_hbm, w_in.at[0]), fetch(w_neigh_hbm, w_in.at[1])]

    def xt_copy(s):
        m = (me + s) % CUTS
        return pltpu.make_async_copy(xt_hbm.at[m], xt.at[m], load.at[16 + s])

    def xt_start(s, _):
        xt_copy(s).start()
        return 0

    lax.fori_loop(1, CUTS + 1, xt_start, 0)
    ld_top = [fetch(final_hbm, raw.at[0]), fetch(third_hbm, raw.at[1])]
    ld_second = [fetch(second_self_hbm, second.at[0]), fetch(second_neigh_hbm, second.at[1])]

    sends = []

    def start(n, src, dst, to):
        pltpu.make_async_remote_copy(
            src_ref=src, dst_ref=dst, send_sem=send.at[n], recv_sem=recv.at[n], device_id=to, device_id_type=MESH
        ).start()

    def link_all(whole, copies):
        n = len(sends)
        sends.append(whole)
        for src, dst, to in copies:
            start(n, src, dst, to)
        return n

    def link(src, dst, to):
        return link_all(src, [(src, dst, to)])

    def pair_of(n, ref):
        return pltpu.make_async_remote_copy(
            src_ref=ref, dst_ref=ref, send_sem=send.at[n], recv_sem=recv.at[n], device_id=sibling, device_id_type=MESH
        )

    def arrived(n, dst):
        pair_of(n, dst).wait_recv()

    for cp in ld_w:
        cp.wait()
    wa[k, me] = w_in[k, :, 0:512]
    wb[k, y, me] = w_in[k, :, pl.ds(pl.multiple_of(512 + y * 128, 128), 128)]
    ld_lists.wait()
    pl.semaphore_wait(barrier, len(peers))

    wbz = [link(wb.at[k, y, me], wb.at[k, y, me], peer(dzh=s)) for s in range(1, 4)]

    def across(j):
        src = wa.at[k, behinds[j]]
        for s in range(1, 4):
            start(wax[s - 1], src, src, peer(dx=s))

    wax = [link_all(wa.at[k, quads[0]], []) for s in range(1, 4)]
    waz = [link(wa.at[k, me], wa.at[k, me], peer(dzh=s)) for s in range(1, 4)]

    across(0)

    def block(m):
        one, zero = jnp.ones((16, R1), BF), jnp.zeros((16, R1), BF)
        wanted = [jnp.broadcast_to(lists[f, pl.ds(m, 1), :], (16, R1)).astype(jnp.int16) for f in range(FAN1)]
        base = lax.broadcasted_iota(jnp.int32, (16, R1), 0).astype(jnp.int16)
        parts = []
        for b in range(R0 // 16):
            row = base + jnp.int16(16 * b)
            v = jnp.where(row == wanted[0], one, zero)
            for f in range(1, FAN1):
                v = v + jnp.where(row == wanted[f], one, zero)
            parts.append(v)
        mean = (dot(xt[m], jnp.concatenate(parts, axis=0)) * (1.0 / FAN1)).astype(BF)
        return xt[m][:, :R1], mean

    def pack(ref, m, own, mean):
        ref[m, 0:48] = own[:, 0:128]
        ref[m, 48:96] = mean[:, 0:128]
        ref[m, 96:144] = jnp.concatenate([own[:, 128:192], mean[:, 128:192]], axis=1)

    def a_pair(s=None):
        here = pl.ds(0, CUTS - 1) if s is None else s - 1
        return pltpu.make_async_remote_copy(
            src_ref=blk_out.at[here], dst_ref=blk_in.at[here], send_sem=a_send.at[0], recv_sem=a_recv.at[0],
            device_id=sibling if s is None else {"dp": d, "cuts": (me + s) % CUTS}, device_id_type=MESH,
        )

    def one(s, _):
        xt_copy(s).wait()
        own, mean = block((me + s) % CUTS)
        pack(blk_out, s - 1, own, mean)

        @pl.when(s < CUTS)
        def _():
            a_pair(s).start()

        @pl.when(s == 6)
        def _():
            for j in range(1, 4):
                arrived(wbz[j - 1], wb.at[k, y, behinds[j]])
            for s in range(1, 4):
                wbx.append(link(wb.at[k, y, quads[0]], wb.at[k, y, quads[0]], peer(dx=s)))

        @pl.when(s == 8)
        def _():
            for j in (1, 3):
                arrived(waz[j - 1], wa.at[k, behinds[j]])
                across(j)

        @pl.when(s == 11)
        def _():
            for s in range(1, 4):
                arrived(wbx[s - 1], wb.at[k, y, quads[-s]])
            for s in range(1, 4):
                wby.append(link(wb.at[k, y], wb.at[k, y], peer(dy=s)))
            wbk.append(link(wb.at[k, y], wb.at[k, y], sibling))

        @pl.when(s == 13)
        def _():
            arrived(waz[1], wa.at[k, behinds[2]])
            across(2)
            wak.append(link(wa.at[k, quads[0]], wa.at[k, quads[0]], sibling))

        return 0

    wbx, wby, wak, wbk = [], [], [], []
    lax.fori_loop(1, CUTS + 1, one, 0)

    for cp in ld_top:
        cp.wait()
    for i in range(2):
        top[i, 144:256] = jnp.zeros((112, HID), BF)
        top[i, 0:CLASSES] = raw[i]
    for cp in ld_idx:
        cp.wait()
    idx[...] = jnp.full((16, 256), -1, jnp.int32)
    for f in range(FAN2):
        idx[f:f + 1, 0:R2] = lists2[f]
    for f in range(FAN3):
        idx[FAN2 + f:FAN2 + f + 1, 0:SEEDS] = lists3[f]
    idx[8:9, 0:SEEDS] = labels[...]
    rows256 = lax.broadcasted_iota(jnp.int32, (256, 256), 0)

    def counting(first, fan):
        counts = jnp.zeros((256, 256), F32)
        for f in range(first, first + fan):
            counts = counts + jnp.where(rows256 == idx[f:f + 1, :], 1.0, 0.0)
        return counts

    counts2t, counts3t = counting(0, FAN2), counting(FAN2, FAN3)
    counts2, counts3 = counts2t.T.astype(BF), counts3t.T.astype(BF)
    counts2t, counts3t = counts2t.astype(BF), counts3t.astype(BF)
    onehot = jnp.where(rows256 == idx[8:9, :], 1.0, 0.0).T[:SEEDS]
    act1[R1:256] = jnp.zeros((256 - R1, HID), BF)
    act2[R2:256] = jnp.zeros((256 - R2, HID), BF)
    back2[R2:256] = jnp.zeros((256 - R2, HID), BF)

    for s in range(1, 4):
        arrived(wax[s - 1], wa.at[k, quads[-s]])
        wak.append(link(wa.at[k, quads[-s]], wa.at[k, quads[-s]], sibling))
    a_pair().wait_recv()
    for s in range(CUTS):
        src, ref, i = (me + CUTS - s) % CUTS, blk_in if s else blk_out, s - 1 if s else CUTS - 1
        here = pl.ds(pl.multiple_of(src * WIDE, WIDE), WIDE)
        tail = ref[i, 96:144]
        at[0, here, 0:128] = ref[i, 0:48]
        at[1, here, 0:128] = ref[i, 48:96]
        at[0, here, 128:192] = tail[:, 0:64]
        at[1, here, 128:192] = tail[:, 64:128]
    sw_a1 = link(at.at[1 - k], ra1, sibling)
    at0, at1 = at[0].T, at[1].T
    for s in range(1, 4):
        frm = (y + 4 - s) % 4
        arrived(wby[s - 1], wb.at[k, frm])
        wbk.append(link(wb.at[k, frm], wb.at[k, frm], sibling))

    for n in range(4):
        if n == 0:
            for s in range(4):
                arrived(wak[s], wa.at[1 - k, quads[-s]])
        if n == 2:
            for s in range(4):
                arrived(wbk[s], wb.at[1 - k, (y + 4 - s) % 4])
        if n < 2:
            w0, w1 = (wa[i, :, :, lanes(n)].reshape(ROWS, 256) for i in range(2))
        else:
            q = 2 * n - 4
            w0, w1 = (
                jnp.concatenate([wb[i, q].reshape(ROWS, 128), wb[i, q + 1].reshape(ROWS, 128)], axis=1)
                for i in range(2)
            )
        v = dot(at0, w0) + dot(at1, w1)
        pre1[:, lanes(n)] = v
        act1[0:R1, lanes(n)] = (v * sigmoid(v)).astype(BF)
    for n in range(4):
        mean2[:, lanes(n)] = (dot(counts2[:R2], act1[:, lanes(n)]) * (1.0 / FAN2)).astype(BF)
    for cp in ld_second:
        cp.wait()
    for n in range(4):
        v = dot(act1[0:R2], second[0, :, lanes(n)]) + dot(mean2[...], second[1, :, lanes(n)])
        pre2[:, lanes(n)] = v
        act2[0:R2, lanes(n)] = (v * sigmoid(v)).astype(BF)
    for n in range(4):
        mean3[:, lanes(n)] = (dot(counts3[:SEEDS], act2[:, lanes(n)]) * (1.0 / FAN3)).astype(BF)
    logits = dot_nt(act2[0:SEEDS], top[0]) + dot_nt(mean3[...], top[1])
    column = lax.broadcasted_iota(jnp.int32, (SEEDS, PADDED), 1)
    expon = jnp.where(column < CLASSES, jnp.exp(logits), 0.0)
    total = jnp.sum(expon, axis=1, keepdims=True)
    each = jnp.log(total) - jnp.sum(logits * onehot, axis=1, keepdims=True)
    loss[...] = jnp.sum(each, axis=0, keepdims=True) * (1.0 / SEEDS)
    g3[...] = ((expon / total - onehot) * (1.0 / SEEDS)).astype(BF)

    sw_g3 = link(g3, rg3, sibling)
    keep3, keep2, give3, give2 = rest_keep
    give3[...] = jnp.where(k == 0, mean3[...], act2[0:SEEDS])
    keep3[...] = jnp.where(k == 0, act2[0:SEEDS], mean3[...])
    sw_a3 = link(give3, ra3, sibling)
    give2[...] = jnp.where(k == 0, mean2[...], act1[0:R2])
    keep2[...] = jnp.where(k == 0, act1[0:R2], mean2[...])
    sw_a2 = link(give2, ra2, sibling)
    for n in range(4):
        back = (dot(g3[...], top[1, :, lanes(n)]) * (1.0 / FAN3)).astype(BF)
        own = dot(g3[...], top[0, :, lanes(n)])
        grad = dot(counts3t[:R2, :SEEDS], back) + jnp.concatenate([own, jnp.zeros((R2 - SEEDS, 256), F32)], axis=0)
        g2[:, lanes(n)] = (grad * slope(pre2[:, lanes(n)])).astype(BF)
    sw_g2 = link(g2, rg2, sibling)

    class Ring:
        def __init__(self, block, add, up, down, relay, direct, comb):
            self.block, self.add, self.up, self.down = block, add, up, down
            self.relay, self.direct, self.comb = relay, direct, comb

        def opposite(self):
            self.n_relay = (
                link(self.block(2, 0), self.relay.at[0], self.up), link(self.block(2, 1), self.relay.at[1], self.down)
            )

        def to_up(self):
            self.n_up = link(self.block(1, 1), self.direct.at[1], self.up)

        def to_down(self):
            self.n_down = link(self.block(3, 0), self.direct.at[0], self.down)

        def pass_on(self):
            self.n_comb = []
            for h, off, to in ((0, 1, self.up), (1, 3, self.down)):
                arrived(self.n_relay[h], self.relay.at[h])
                self.add(self.relay.at[h], (self.relay.at[h], self.block(off, h)))
                self.n_comb.append(link(self.relay.at[h], self.comb.at[h], to))

        def finish(self, out):
            for h, n in ((0, self.n_down), (1, self.n_up)):
                arrived(self.n_comb[h], self.comb.at[h])
                arrived(n, self.direct.at[h])
                self.add(out(h), (self.block(0, h), self.comb.at[h], self.direct.at[h]))

    def add_leading(dst, parts):
        def body(i, _):
            v = parts[0][i].astype(F32)
            for p in parts[1:]:
                v = v + p[i].astype(F32)
            dst[i] = v.astype(BF)
            return 0

        lax.fori_loop(0, dst.shape[0], body, 0)

    class Chunk:
        def __init__(self, sizes, bufs, out, back):
            self.rows, self.out, self.back = sizes, out, back
            (
                self.s1, self.s2, rel1, dir1, com1, rel2, dir2, com2, self.t1, self.t2, self.q1, self.q2, self.u,
                self.sz, self.rz1, self.tz, self.rt,
            ) = bufs
            self.y = Ring(
                lambda off, h: self.s1.at[ys[off], pl.ds(8 * h, 8)], add_leading, peer(dy=1), peer(dy=3), rel1, dir1, com1
            )
            self.x = Ring(
                lambda off, h: self.s2.at[:, pl.ds(xs[off] * 4 + 2 * h, 2)],
                add_leading, peer(dx=1), peer(dx=3), rel2, dir2, com2,
            )

        def first_y_done(self):
            self.y.finish(lambda h: self.t1.at[pl.ds(8 * h, 8)])
            self.n1 = link_all(self.q1, [(self.t1.at[quads[s]], self.q1.at[s - 1], peer(dx=s)) for s in range(1, 4)])

        def first_x_done(self):
            self.x.finish(lambda h: self.t2.at[:, pl.ds(2 * h, 2)])
            self.n2 = link_all(self.q2, [(self.t2.at[ys[s]], self.q2.at[s - 1], peer(dy=s)) for s in range(1, 4)])

        def fill_z(self, n, v):
            for i in range(CUTS):
                for h in range(2):
                    self.sz[h, i % 4, i // 4, n] = v[i, :, lanes(h, 128)]

        def z_first(self):
            far = [(zl * 4 + zh + s) % 8 for s in range(1, 8)]
            self.n6 = link_all(
                self.rz1,
                [(self.sz.at[p // 4, p % 4], self.rz1.at[s], device(x, y, p % 4, p // 4, k)) for s, p in enumerate(far)],
            )

        def z_sum(self):
            arrived(self.n6, self.rz1)
            for i in range(4):
                v = self.sz[zl, zh, i].astype(F32)
                for s in range(7):
                    v = v + self.rz1[s, i].astype(F32)
                self.tz[i] = v.astype(BF)
            self.n7 = link_all(
                self.rt,
                [
                    (self.tz.at[xs[q // 4], ys[q % 4]], self.rt.at[q - 1], peer(dx=q // 4, dy=q % 4))
                    for q in range(1, 16)
                ],
            )

        def second_done(self, rz):
            r1, r2, _ = self.rows
            for lo, hi, number, t, q in (
                (0, r1, self.n1, lambda h: self.t1[x * 4 + h], self.q1),
                (r1, r1 + r2, self.n2, lambda h: self.t2[y, h], self.q2),
            ):
                arrived(number, q)
                for h in range(4):
                    v = t(h).astype(F32)
                    for s in range(3):
                        v = v + q[s, h].astype(F32)
                    v = v.astype(BF)
                    self.u[0, h, lo:hi] = v[:, 0:128]
                    self.u[1, h, lo:hi] = v[:, 128:256]
            self.rz = rz
            far = [(zl * 4 + zh + s) % 8 for s in range(1, 8)]
            self.n3 = link_all(
                rz, [(self.u.at[p // 4, p % 4], rz.at[s], device(x, y, p % 4, p // 4, k)) for s, p in enumerate(far)]
            )

        def third_done(self):
            v = self.u[zl, zh].astype(F32)
            arrived(self.n3, self.rz)
            for s in range(7):
                v = v + self.rz[s].astype(F32)
            self.mine = y * 2 + zl
            piece = self.out.at[k, self.mine]
            rows = self.rows[0] + self.rows[1]
            self.out[k, self.mine, 0:rows] = v.astype(BF)
            arrived(self.n7, self.rt)
            v = self.tz[x, y].astype(F32)
            for s in range(15):
                v = v + self.rt[s].astype(F32)
            self.out[k, self.mine, rows:rows + 16] = v.astype(BF)
            far = [(self.mine + s) % 8 for s in range(1, 8)]
            self.n4 = link_all(
                self.back, [(piece, self.back.at[s], device(x, p // 2, zh, p % 2, k)) for s, p in enumerate(far)]
            )

        def gathered(self):
            arrived(self.n4, self.back)
            for s in range(1, 8):
                self.out[k, (self.mine + 8 - s) % 8] = self.back[s - 1]
            self.n5 = link(self.out.at[k], self.out.at[k], sibling)

        def done(self):
            arrived(self.n5, self.out.at[1 - k])

    upper, lower = Chunk(UPPER, bufs_a, out_a, rest_rz[2]), Chunk(LOWER, bufs_b, out_b, rest_rz[3])
    order = (2, 1, 3, 0)

    arrived(sw_g3, rg3)
    arrived(sw_a3, ra3)
    third = (dot(keep3[...].T, g3[...]) + dot(ra3[...].T, rg3[...])).astype(BF).reshape(CUTS, 4, 16, 256)
    for j in range(4):
        upper.fill_z(j, third[:, j])
    upper.z_first()
    keep_t = keep2[...].T
    arrived(sw_a2, ra2)
    sib_t = ra2[...].T
    for n in range(4):
        back2[0:R2, lanes(n)] = (dot_nt(g2[...], second[1, lanes(n), :]) * (1.0 / FAN2)).astype(BF)
    arrived(sw_g2, rg2)
    for off in order:
        n = ys[off]
        p = (dot(keep_t, g2[:, lanes(n)]) + dot(sib_t, rg2[:, lanes(n)])).astype(BF).reshape(CUTS, 64, 256)
        upper.s1[n] = p[:, 0:32]
        upper.s2[n] = p[:, 32:64]
        if off == 2:
            upper.y.opposite()
        if off == 1:
            upper.y.to_up()
        if off == 3:
            upper.y.to_down()
    upper.x.opposite()
    upper.x.to_up()
    upper.x.to_down()

    for n in range(4):
        own = dot_nt(g2[...], second[0, lanes(n), :])
        grad = dot(counts2t[:R1], back2[:, lanes(n)]) + jnp.concatenate(
            [own, jnp.zeros((R1 - R2, 256), F32)], axis=0
        )
        g1[:, lanes(n)] = (grad * slope(pre1[:, lanes(n)])).astype(BF)
    sw_g1 = link(g1, rg1, sibling)
    arrived(sw_a1, ra1)
    arrived(sw_g1, rg1)
    for off in order:
        n = ys[off]
        p = (dot(at[k], g1[:, lanes(n)]) + dot(ra1[...], rg1[:, lanes(n)])).astype(BF).reshape(CUTS, 48, 256)
        lower.s1[n] = p[:, 0:16]
        lower.s2[n] = p[:, 16:32]
        lower.fill_z(n, p[:, 32:48])
        if off == 2:
            lower.y.opposite()
        if off == 1:
            lower.y.to_up()
            upper.y.pass_on()
        if off == 3:
            lower.y.to_down()
            upper.x.pass_on()
    lower.z_first()
    lower.x.opposite()
    lower.x.to_up()
    lower.x.to_down()
    upper.first_y_done()
    upper.first_x_done()
    upper.z_sum()
    lower.y.pass_on()
    lower.x.pass_on()
    upper.second_done(rest_rz[0])
    lower.first_y_done()
    lower.first_x_done()
    lower.second_done(rest_rz[1])
    lower.z_sum()
    upper.third_done()
    lower.third_done()
    upper.gathered()
    lower.gathered()
    upper.done()
    lower.done()

    for n, ref in enumerate(sends):
        pair_of(n, ref).wait_send()
    a_pair().wait_send()


def step(*operands):
    dma = pltpu.SemaphoreType.DMA
    vm = lambda *shape: pltpu.VMEM(shape, BF)
    vf = lambda *shape: pltpu.VMEM(shape, F32)
    vi = lambda *shape: pltpu.VMEM(shape, jnp.int32)

    def chunk(sizes):
        r1, r2, r3 = sizes
        return [
            vm(4, CUTS, r1, 256), vm(4, CUTS, r2, 256),
            vm(2, 8, r1, 256), vm(2, 8, r1, 256), vm(2, 8, r1, 256),
            vm(2, 4, 2, r2, 256), vm(2, 4, 2, r2, 256), vm(2, 4, 2, r2, 256),
            vm(CUTS, r1, 256), vm(4, 4, r2, 256),
            vm(3, 4, r1, 256), vm(3, 4, r2, 256),
            vm(2, 4, r1 + r2, 128),
            vm(2, 4, 4, 4, r3, 128), vm(7, 4, 4, r3, 128), vm(4, 4, r3, 128), vm(15, r3, 128),
        ]

    return pl.pallas_call(
        kernel,
        out_shape=(
            jax.ShapeDtypeStruct((1, 1), F32),
            jax.ShapeDtypeStruct((2, 8, sum(UPPER), 128), BF),
            jax.ShapeDtypeStruct((2, 8, sum(LOWER), 128), BF),
        ),
        in_specs=[ANY] * 11,
        out_specs=(VMEM,) * 3,
        scratch_shapes=[
            vi(FAN1, CUTS, R1), vi(FAN2, 1, R2), vi(FAN3, 1, SEEDS), vi(1, SEEDS), vi(16, 256), vm(CUTS, WIDE, R0), vm(2, WIDE, HID), vm(2, HID, HID),
            vm(2, CLASSES, HID), vm(2, PADDED, HID),
            vm(CUTS, 144, 128), vm(CUTS - 1, 144, 128), vm(2, CUTS, WIDE, 512), vm(2, 4, CUTS, WIDE, 128), vm(2, ROWS, R1),
            vf(R1, HID), vm(256, HID), vm(R2, HID), vf(R2, HID), vm(256, HID), vm(SEEDS, HID), vm(256, HID),
            vm(R1, HID), vm(R2, HID), vm(SEEDS, PADDED),
            vm(ROWS, R1), vm(R2, HID), vm(SEEDS, HID), vm(R1, HID), vm(R2, HID), vm(SEEDS, PADDED),
        ]
        + chunk(UPPER)
        + chunk(LOWER)
        + [
            vm(SEEDS, HID), vm(R2, HID), vm(SEEDS, HID), vm(R2, HID),
            vm(7, sum(UPPER[:2]), 128), vm(7, sum(LOWER[:2]), 128), vm(7, sum(UPPER), 128), vm(7, sum(LOWER), 128),
            dma((33,)), dma((SLOTS,)), dma((SLOTS,)), dma((1,)), dma((1,)),
        ],
        compiler_params=pltpu.CompilerParams(
            collective_id=1, has_side_effects=True, vmem_limit_bytes=56 * 2**20
        ),
    )(*operands)


def finish_kernel(upper, lower, first_self, first_neigh, second_self, second_neigh, third_self, third_neigh):
    for k, first, second, third in (
        (0, first_self, second_self, third_self), (1, first_neigh, second_neigh, third_neigh)
    ):
        for g in range(8):
            first[:, lanes(g, 128)] = lower[k, g].astype(F32)
            second[:, lanes(g, 128)] = upper[k, g, 0:64].astype(F32)
            lo = (g % 2) * 128
            width = min(128, CLASSES - lo)
            third[g // 2 * 16:g // 2 * 16 + 16, lo:lo + width] = upper[k, g, 64:80, 0:width].astype(F32)


def finish(upper, lower):
    shapes = ((48, HID), (48, HID), (64, HID), (64, HID), (64, CLASSES), (64, CLASSES))
    return pl.pallas_call(
        finish_kernel,
        out_shape=tuple(jax.ShapeDtypeStruct(s, F32) for s in shapes),
        in_specs=[VMEM] * 2,
        out_specs=(VMEM,) * 6,
    )(upper, lower)


def per_device(
    features, lists_one, lists_two, lists_three, labels, initial_node_weight, initial_neighbour_weight,
    second_self, second_neigh, final_node_weight, third_neigh,
):
    xt = jnp.swapaxes(features[0], 1, 2)
    lists = jnp.transpose(lists_one[0], (2, 0, 1))

    loss, upper, lower = step(
        lists, xt, initial_node_weight, initial_neighbour_weight, second_self, second_neigh,
        final_node_weight.T, third_neigh.T,
        jnp.transpose(lists_two[0], (2, 0, 1)), jnp.transpose(lists_three[0], (2, 0, 1)), labels[0],
    )
    return (loss,) + tuple(finish(upper, lower))


def solution(mesh):
    return jax.shard_map(
        per_device,
        mesh=mesh,
        in_specs=(
            P("dp", None, None, "cuts"),
            P("dp", None, None, None),
            P("dp", "cuts", None, None),
            P("dp", "cuts", None, None),
            P("dp", "cuts", None),
            P("cuts", None),
            P("cuts", None),
            P(), P(), P(), P(),
        ),
        out_specs=(P("dp", "cuts"),) + (P("cuts", None),) * 6,
        check_vma=False,
    )
```

```python
import jax
import jax.numpy as jnp
from jax import lax
from jax.experimental import pallas as pl
from jax.experimental.pallas import tpu as pltpu
from jax.sharding import PartitionSpec as P

MESH = pl.DeviceIdType.MESH
BF = jnp.bfloat16
F32 = jnp.float32
FAN1 = 5
FAN2 = 5
FAN3 = 3
R0 = 1024
R1 = 192
R2 = 160
SEEDS = 128
HID = 1024
CUTS = 16
WIDE = 48
ROWS = CUTS * WIDE
CLASSES = 153
PADDED = 256
VMEM = pl.BlockSpec(memory_space=pltpu.VMEM)
ANY = pl.BlockSpec(memory_space=pl.ANY)
SLOTS = 67
UPPER = (32, 32, 16)
LOWER = (16, 16, 16)


def dot(a, b):
    return jnp.dot(a, b, preferred_element_type=F32)


def dot_nt(a, b):
    return lax.dot_general(a, b, (((1,), (1,)), ((), ())), preferred_element_type=F32)


def sigmoid(v):
    return 1.0 / (1.0 + jnp.exp(-v))


def slope(v):
    s = sigmoid(v)
    return s * (1.0 + v * (1.0 - s))


def lanes(n, width=256):
    if isinstance(n, int):
        return slice(n * width, (n + 1) * width)
    return pl.ds(pl.multiple_of(n * width, width), width)


def kernel(
    lists_hbm, xt_hbm, w_self_hbm, w_neigh_hbm, second_self_hbm, second_neigh_hbm, final_hbm, third_hbm,
    lists2_hbm, lists3_hbm, labels_hbm,
    loss, out_a, out_b,
    lists, lists2, lists3, labels, idx, xt, w_in, second, raw, top,
    blk_out, blk_in, wa, wb, at,
    pre1, act1, mean2, pre2, act2, mean3, back2, g1, g2, g3,
    ra1, ra2, ra3, rg1, rg2, rg3,
    *rest,
):
    bufs_a, bufs_b = rest[:17], rest[17:34]
    rest_keep, rest_rz = rest[34:38], rest[38:42]
    load, send, recv, a_send, a_recv = rest[42:]
    d, c = lax.axis_index("dp"), lax.axis_index("cuts")
    x, y, zh, zl, k = c // 4, d // 4, c % 4, (d // 2) % 2, d % 2
    me = c

    def device(px, py, pzh, pzl, pk):
        return {"dp": (py * 2 + pzl) * 2 + pk, "cuts": px * 4 + pzh}

    def peer(dx=0, dy=0, dzh=0, dzl=0, dk=0):
        return device((x + dx) % 4, (y + dy) % 4, (zh + dzh) % 4, (zl + dzl) % 2, (k + dk) % 2)

    sibling = peer(dk=1)
    xs = [(x + s) % 4 for s in range(4)]
    quads = [pl.ds(pl.multiple_of(v * 4, 4), 4) for v in xs]
    behinds = [x * 4 + (zh + 4 - j) % 4 for j in range(4)]
    ys = [(y + s) % 4 for s in range(4)]

    barrier = pltpu.get_barrier_semaphore()
    peers = [peer(dx=s // 4, dzh=s % 4) for s in range(1, 16)]
    peers += [peer(dy=s // 2, dzl=s % 2) for s in range(1, 8)]
    peers += [peer(dzh=s, dzl=1) for s in range(1, 4)]
    peers += [peer(dx=i, dy=j) for i in range(1, 4) for j in range(1, 4)]
    peers += [sibling]
    for p in peers:
        pl.semaphore_signal(barrier, 1, device_id=p, device_id_type=MESH)

    count = [0]

    def fetch(src, dst):
        cp = pltpu.make_async_copy(src, dst, load.at[count[0]])
        count[0] += 1
        cp.start()
        return cp

    ld_lists = fetch(lists_hbm, lists)
    ld_idx = [fetch(lists2_hbm, lists2), fetch(lists3_hbm, lists3), fetch(labels_hbm, labels)]
    ld_w = [fetch(w_self_hbm, w_in.at[0]), fetch(w_neigh_hbm, w_in.at[1])]

    def ahead(s):
        q = s - 1
        far = 1 - q // 12
        return far * (q // 3) + (1 - far) * (q - 11), far * (1 + q % 3)

    def cut_ahead(s):
        dx, dz = ahead(s)
        return (x + dx) % 4 * 4 + (zh + dz) % 4

    def xt_copy(s):
        m = cut_ahead(s)
        return pltpu.make_async_copy(xt_hbm.at[m], xt.at[m], load.at[16 + s])

    def xt_start(s, _):
        xt_copy(s).start()
        return 0

    lax.fori_loop(1, CUTS + 1, xt_start, 0)
    ld_top = [fetch(final_hbm, raw.at[0]), fetch(third_hbm, raw.at[1])]
    ld_second = [fetch(second_self_hbm, second.at[0]), fetch(second_neigh_hbm, second.at[1])]

    sends = []

    def start(n, src, dst, to):
        pltpu.make_async_remote_copy(
            src_ref=src, dst_ref=dst, send_sem=send.at[n], recv_sem=recv.at[n], device_id=to, device_id_type=MESH
        ).start()

    def link_all(whole, copies):
        n = len(sends)
        sends.append(whole)
        for src, dst, to in copies:
            start(n, src, dst, to)
        return n

    def link(src, dst, to):
        return link_all(src, [(src, dst, to)])

    def pair_of(n, ref):
        return pltpu.make_async_remote_copy(
            src_ref=ref, dst_ref=ref, send_sem=send.at[n], recv_sem=recv.at[n], device_id=sibling, device_id_type=MESH
        )

    def arrived(n, dst):
        pair_of(n, dst).wait_recv()

    for cp in ld_w:
        cp.wait()
    wa[k, me] = w_in[k, :, 0:512]
    wb[k, y, me] = w_in[k, :, pl.ds(pl.multiple_of(512 + y * 128, 128), 128)]
    ld_lists.wait()
    def block(m):
        one, zero = jnp.ones((16, R1), BF), jnp.zeros((16, R1), BF)
        wanted = [jnp.broadcast_to(lists[f, pl.ds(m, 1), :], (16, R1)).astype(jnp.int16) for f in range(FAN1)]
        base = lax.broadcasted_iota(jnp.int32, (16, R1), 0).astype(jnp.int16)
        parts = []
        for b in range(R0 // 16):
            row = base + jnp.int16(16 * b)
            v = jnp.where(row == wanted[0], one, zero)
            for f in range(1, FAN1):
                v = v + jnp.where(row == wanted[f], one, zero)
            parts.append(v)
        mean = (dot(xt[m], jnp.concatenate(parts, axis=0)) * (1.0 / FAN1)).astype(BF)
        return xt[m][:, :R1], mean

    def pack(ref, m, own, mean):
        ref[m, 0:48] = own[:, 0:128]
        ref[m, 48:96] = mean[:, 0:128]
        ref[m, 96:144] = jnp.concatenate([own[:, 128:192], mean[:, 128:192]], axis=1)

    def prepare(s, _):
        xt_copy(s).wait()
        own, mean = block(cut_ahead(s))
        pack(blk_out, s - 1, own, mean)
        return 0

    lax.fori_loop(1, 4, prepare, 0)
    pl.semaphore_wait(barrier, len(peers))

    wbz = [link(wb.at[k, y, me], wb.at[k, y, me], peer(dzh=s)) for s in range(1, 4)]

    def across(j):
        src = wa.at[k, behinds[j]]
        for s in range(1, 4):
            start(wax[s - 1], src, src, peer(dx=s))

    wax = [link_all(wa.at[k, quads[0]], []) for s in range(1, 4)]
    waz = [link(wa.at[k, me], wa.at[k, me], peer(dzh=s)) for s in range(1, 4)]

    across(0)

    def a_pair(s=None):
        here = pl.ds(0, CUTS - 1) if s is None else s - 1
        return pltpu.make_async_remote_copy(
            src_ref=blk_out.at[here], dst_ref=blk_in.at[here], send_sem=a_send.at[0], recv_sem=a_recv.at[0],
            device_id=sibling if s is None else {"dp": d, "cuts": cut_ahead(s)}, device_id_type=MESH,
        )

    def one(s, _):
        @pl.when(s >= 4)
        def _():
            prepare(s, 0)

        @pl.when(s < CUTS)
        def _():
            a_pair(s).start()

        @pl.when(s == 6)
        def _():
            for j in range(1, 4):
                arrived(wbz[j - 1], wb.at[k, y, behinds[j]])
            for s in range(1, 4):
                wbx.append(link(wb.at[k, y, quads[0]], wb.at[k, y, quads[0]], peer(dx=s)))

        @pl.when(s == 8)
        def _():
            for j in (1, 3):
                arrived(waz[j - 1], wa.at[k, behinds[j]])
                across(j)

        @pl.when(s == 11)
        def _():
            for s in range(1, 4):
                arrived(wbx[s - 1], wb.at[k, y, quads[-s]])
            for s in range(1, 4):
                wby.append(link(wb.at[k, y], wb.at[k, y], peer(dy=s)))
            wbk.append(link(wb.at[k, y], wb.at[k, y], sibling))

        @pl.when(s == 13)
        def _():
            arrived(waz[1], wa.at[k, behinds[2]])
            across(2)
            wak.append(link(wa.at[k, quads[0]], wa.at[k, quads[0]], sibling))

        return 0

    wbx, wby, wak, wbk = [], [], [], []
    lax.fori_loop(1, CUTS + 1, one, 0)

    for cp in ld_top:
        cp.wait()
    for i in range(2):
        top[i, 144:256] = jnp.zeros((112, HID), BF)
        top[i, 0:CLASSES] = raw[i]
    for cp in ld_idx:
        cp.wait()
    idx[...] = jnp.full((16, 256), -1, jnp.int32)
    for f in range(FAN2):
        idx[f:f + 1, 0:R2] = lists2[f]
    for f in range(FAN3):
        idx[FAN2 + f:FAN2 + f + 1, 0:SEEDS] = lists3[f]
    idx[8:9, 0:SEEDS] = labels[...]
    rows256 = lax.broadcasted_iota(jnp.int32, (256, 256), 0)

    def counting(first, fan):
        counts = jnp.zeros((256, 256), F32)
        for f in range(first, first + fan):
            counts = counts + jnp.where(rows256 == idx[f:f + 1, :], 1.0, 0.0)
        return counts

    counts2t, counts3t = counting(0, FAN2), counting(FAN2, FAN3)
    counts2, counts3 = counts2t.T.astype(BF), counts3t.T.astype(BF)
    counts2t, counts3t = counts2t.astype(BF), counts3t.astype(BF)
    onehot = jnp.where(rows256 == idx[8:9, :], 1.0, 0.0).T[:SEEDS]
    act1[R1:256] = jnp.zeros((256 - R1, HID), BF)
    act2[R2:256] = jnp.zeros((256 - R2, HID), BF)
    back2[R2:256] = jnp.zeros((256 - R2, HID), BF)

    for s in range(1, 4):
        arrived(wax[s - 1], wa.at[k, quads[-s]])
        wak.append(link(wa.at[k, quads[-s]], wa.at[k, quads[-s]], sibling))
    a_pair().wait_recv()
    for s in range(1, CUTS + 1):
        dx, dz = ahead(s)
        src, ref, i = (x + 8 - dx) % 4 * 4 + (zh + 4 - dz) % 4, blk_in if s < CUTS else blk_out, s - 1
        here = pl.ds(pl.multiple_of(src * WIDE, WIDE), WIDE)
        tail = ref[i, 96:144]
        at[0, here, 0:128] = ref[i, 0:48]
        at[1, here, 0:128] = ref[i, 48:96]
        at[0, here, 128:192] = tail[:, 0:64]
        at[1, here, 128:192] = tail[:, 64:128]
    sw_a1 = link(at.at[1 - k], ra1, sibling)
    at0, at1 = at[0].T, at[1].T
    for s in range(1, 4):
        frm = (y + 4 - s) % 4
        arrived(wby[s - 1], wb.at[k, frm])
        wbk.append(link(wb.at[k, frm], wb.at[k, frm], sibling))

    for n in range(4):
        if n == 0:
            for s in range(4):
                arrived(wak[s], wa.at[1 - k, quads[-s]])
        if n == 2:
            for s in range(4):
                arrived(wbk[s], wb.at[1 - k, (y + 4 - s) % 4])
        if n < 2:
            w0, w1 = (wa[i, :, :, lanes(n)].reshape(ROWS, 256) for i in range(2))
        else:
            q = 2 * n - 4
            w0, w1 = (
                jnp.concatenate([wb[i, q].reshape(ROWS, 128), wb[i, q + 1].reshape(ROWS, 128)], axis=1)
                for i in range(2)
            )
        v = dot(at0, w0) + dot(at1, w1)
        pre1[:, lanes(n)] = v
        act1[0:R1, lanes(n)] = (v * sigmoid(v)).astype(BF)
    for n in range(4):
        mean2[:, lanes(n)] = (dot(counts2[:R2], act1[:, lanes(n)]) * (1.0 / FAN2)).astype(BF)
    for cp in ld_second:
        cp.wait()
    for n in range(4):
        v = dot(act1[0:R2], second[0, :, lanes(n)]) + dot(mean2[...], second[1, :, lanes(n)])
        pre2[:, lanes(n)] = v
        act2[0:R2, lanes(n)] = (v * sigmoid(v)).astype(BF)
    for n in range(4):
        mean3[:, lanes(n)] = (dot(counts3[:SEEDS], act2[:, lanes(n)]) * (1.0 / FAN3)).astype(BF)
    logits = dot_nt(act2[0:SEEDS], top[0]) + dot_nt(mean3[...], top[1])
    column = lax.broadcasted_iota(jnp.int32, (SEEDS, PADDED), 1)
    expon = jnp.where(column < CLASSES, jnp.exp(logits), 0.0)
    total = jnp.sum(expon, axis=1, keepdims=True)
    each = jnp.log(total) - jnp.sum(logits * onehot, axis=1, keepdims=True)
    loss[...] = jnp.sum(each, axis=0, keepdims=True) * (1.0 / SEEDS)
    g3[...] = ((expon / total - onehot) * (1.0 / SEEDS)).astype(BF)

    sw_g3 = link(g3, rg3, sibling)
    keep3, keep2, give3, give2 = rest_keep
    give3[...] = jnp.where(k == 0, mean3[...], act2[0:SEEDS])
    keep3[...] = jnp.where(k == 0, act2[0:SEEDS], mean3[...])
    sw_a3 = link(give3, ra3, sibling)
    give2[...] = jnp.where(k == 0, mean2[...], act1[0:R2])
    keep2[...] = jnp.where(k == 0, act1[0:R2], mean2[...])
    sw_a2 = link(give2, ra2, sibling)
    for n in range(4):
        back = (dot(g3[...], top[1, :, lanes(n)]) * (1.0 / FAN3)).astype(BF)
        own = dot(g3[...], top[0, :, lanes(n)])
        grad = dot(counts3t[:R2, :SEEDS], back) + jnp.concatenate([own, jnp.zeros((R2 - SEEDS, 256), F32)], axis=0)
        g2[:, lanes(n)] = (grad * slope(pre2[:, lanes(n)])).astype(BF)
    sw_g2 = link(g2, rg2, sibling)

    class Ring:
        def __init__(self, block, add, up, down, relay, direct, comb):
            self.block, self.add, self.up, self.down = block, add, up, down
            self.relay, self.direct, self.comb = relay, direct, comb

        def opposite(self):
            self.n_relay = (
                link(self.block(2, 0), self.relay.at[0], self.up), link(self.block(2, 1), self.relay.at[1], self.down)
            )

        def to_up(self):
            self.n_up = link(self.block(1, 1), self.direct.at[1], self.up)

        def to_down(self):
            self.n_down = link(self.block(3, 0), self.direct.at[0], self.down)

        def pass_on(self):
            self.n_comb = []
            for h, off, to in ((0, 1, self.up), (1, 3, self.down)):
                arrived(self.n_relay[h], self.relay.at[h])
                self.add(self.relay.at[h], (self.relay.at[h], self.block(off, h)))
                self.n_comb.append(link(self.relay.at[h], self.comb.at[h], to))

        def finish(self, out):
            for h, n in ((0, self.n_down), (1, self.n_up)):
                arrived(self.n_comb[h], self.comb.at[h])
                arrived(n, self.direct.at[h])
                self.add(out(h), (self.block(0, h), self.comb.at[h], self.direct.at[h]))

    def add_leading(dst, parts):
        def body(i, _):
            v = parts[0][i].astype(F32)
            for p in parts[1:]:
                v = v + p[i].astype(F32)
            dst[i] = v.astype(BF)
            return 0

        lax.fori_loop(0, dst.shape[0], body, 0)

    class Chunk:
        def __init__(self, sizes, bufs, out, back):
            self.rows, self.out, self.back = sizes, out, back
            (
                self.s1, self.s2, rel1, dir1, com1, rel2, dir2, com2, self.t1, self.t2, self.q1, self.q2, self.u,
                self.sz, self.rz1, self.tz, self.rt,
            ) = bufs
            self.y = Ring(
                lambda off, h: self.s1.at[ys[off], pl.ds(8 * h, 8)], add_leading, peer(dy=1), peer(dy=3), rel1, dir1, com1
            )
            self.x = Ring(
                lambda off, h: self.s2.at[:, pl.ds(xs[off] * 4 + 2 * h, 2)],
                add_leading, peer(dx=1), peer(dx=3), rel2, dir2, com2,
            )

        def first_y_done(self):
            self.y.finish(lambda h: self.t1.at[pl.ds(8 * h, 8)])
            self.n1 = link_all(self.q1, [(self.t1.at[quads[s]], self.q1.at[s - 1], peer(dx=s)) for s in range(1, 4)])

        def first_x_done(self):
            self.x.finish(lambda h: self.t2.at[:, pl.ds(2 * h, 2)])
            self.n2 = link_all(self.q2, [(self.t2.at[ys[s]], self.q2.at[s - 1], peer(dy=s)) for s in range(1, 4)])

        def fill_z(self, n, v):
            for i in range(CUTS):
                for h in range(2):
                    self.sz[h, i % 4, i // 4, n] = v[i, :, lanes(h, 128)]

        def z_first(self):
            far = [(zl * 4 + zh + s) % 8 for s in range(1, 8)]
            self.n6 = link_all(
                self.rz1,
                [(self.sz.at[p // 4, p % 4], self.rz1.at[s], device(x, y, p % 4, p // 4, k)) for s, p in enumerate(far)],
            )

        def z_sum(self):
            arrived(self.n6, self.rz1)
            for i in range(4):
                v = self.sz[zl, zh, i].astype(F32)
                for s in range(7):
                    v = v + self.rz1[s, i].astype(F32)
                self.tz[i] = v.astype(BF)
            self.n7 = link_all(
                self.rt,
                [
                    (self.tz.at[xs[q // 4], ys[q % 4]], self.rt.at[q - 1], peer(dx=q // 4, dy=q % 4))
                    for q in range(1, 16)
                ],
            )

        def second_done(self, rz):
            r1, r2, _ = self.rows
            for lo, hi, number, t, q in (
                (0, r1, self.n1, lambda h: self.t1[x * 4 + h], self.q1),
                (r1, r1 + r2, self.n2, lambda h: self.t2[y, h], self.q2),
            ):
                arrived(number, q)
                for h in range(4):
                    v = t(h).astype(F32)
                    for s in range(3):
                        v = v + q[s, h].astype(F32)
                    v = v.astype(BF)
                    self.u[0, h, lo:hi] = v[:, 0:128]
                    self.u[1, h, lo:hi] = v[:, 128:256]
            self.rz = rz
            far = [(zl * 4 + zh + s) % 8 for s in range(1, 8)]
            self.n3 = link_all(
                rz, [(self.u.at[p // 4, p % 4], rz.at[s], device(x, y, p % 4, p // 4, k)) for s, p in enumerate(far)]
            )

        def third_done(self):
            v = self.u[zl, zh].astype(F32)
            arrived(self.n3, self.rz)
            for s in range(7):
                v = v + self.rz[s].astype(F32)
            self.mine = y * 2 + zl
            piece = self.out.at[k, self.mine]
            rows = self.rows[0] + self.rows[1]
            self.out[k, self.mine, 0:rows] = v.astype(BF)
            arrived(self.n7, self.rt)
            v = self.tz[x, y].astype(F32)
            for s in range(15):
                v = v + self.rt[s].astype(F32)
            self.out[k, self.mine, rows:rows + 16] = v.astype(BF)
            far = [(self.mine + s) % 8 for s in range(1, 8)]
            self.n4 = link_all(
                self.back, [(piece, self.back.at[s], device(x, p // 2, zh, p % 2, k)) for s, p in enumerate(far)]
            )

        def gathered(self):
            arrived(self.n4, self.back)
            for s in range(1, 8):
                self.out[k, (self.mine + 8 - s) % 8] = self.back[s - 1]
            self.n5 = link(self.out.at[k], self.out.at[k], sibling)

        def done(self):
            arrived(self.n5, self.out.at[1 - k])

    upper, lower = Chunk(UPPER, bufs_a, out_a, rest_rz[2]), Chunk(LOWER, bufs_b, out_b, rest_rz[3])
    order = (2, 1, 3, 0)

    arrived(sw_g3, rg3)
    arrived(sw_a3, ra3)
    third = (dot(keep3[...].T, g3[...]) + dot(ra3[...].T, rg3[...])).astype(BF).reshape(CUTS, 4, 16, 256)
    for j in range(4):
        upper.fill_z(j, third[:, j])
    upper.z_first()
    keep_t = keep2[...].T
    arrived(sw_a2, ra2)
    sib_t = ra2[...].T
    for n in range(4):
        back2[0:R2, lanes(n)] = (dot_nt(g2[...], second[1, lanes(n), :]) * (1.0 / FAN2)).astype(BF)
    arrived(sw_g2, rg2)
    for off in order:
        n = ys[off]
        p = (dot(keep_t, g2[:, lanes(n)]) + dot(sib_t, rg2[:, lanes(n)])).astype(BF).reshape(CUTS, 64, 256)
        upper.s1[n] = p[:, 0:32]
        upper.s2[n] = p[:, 32:64]
        if off == 2:
            upper.y.opposite()
        if off == 1:
            upper.y.to_up()
        if off == 3:
            upper.y.to_down()
    upper.x.opposite()
    upper.x.to_up()
    upper.x.to_down()

    for n in range(4):
        own = dot_nt(g2[...], second[0, lanes(n), :])
        grad = dot(counts2t[:R1], back2[:, lanes(n)]) + jnp.concatenate(
            [own, jnp.zeros((R1 - R2, 256), F32)], axis=0
        )
        g1[:, lanes(n)] = (grad * slope(pre1[:, lanes(n)])).astype(BF)
    sw_g1 = link(g1, rg1, sibling)
    arrived(sw_a1, ra1)
    arrived(sw_g1, rg1)
    for off in order:
        n = ys[off]
        p = (dot(at[k], g1[:, lanes(n)]) + dot(ra1[...], rg1[:, lanes(n)])).astype(BF).reshape(CUTS, 48, 256)
        lower.s1[n] = p[:, 0:16]
        lower.s2[n] = p[:, 16:32]
        lower.fill_z(n, p[:, 32:48])
        if off == 2:
            lower.y.opposite()
        if off == 1:
            lower.y.to_up()
            upper.y.pass_on()
        if off == 3:
            lower.y.to_down()
            upper.x.pass_on()
    lower.z_first()
    lower.x.opposite()
    lower.x.to_up()
    lower.x.to_down()
    upper.first_y_done()
    upper.first_x_done()
    upper.z_sum()
    lower.y.pass_on()
    lower.x.pass_on()
    upper.second_done(rest_rz[0])
    lower.first_y_done()
    lower.first_x_done()
    lower.second_done(rest_rz[1])
    lower.z_sum()
    upper.third_done()
    lower.third_done()
    upper.gathered()
    lower.gathered()
    upper.done()
    lower.done()

    for n, ref in enumerate(sends):
        pair_of(n, ref).wait_send()
    a_pair().wait_send()


def step(*operands):
    dma = pltpu.SemaphoreType.DMA
    vm = lambda *shape: pltpu.VMEM(shape, BF)
    vf = lambda *shape: pltpu.VMEM(shape, F32)
    vi = lambda *shape: pltpu.VMEM(shape, jnp.int32)

    def chunk(sizes):
        r1, r2, r3 = sizes
        return [
            vm(4, CUTS, r1, 256), vm(4, CUTS, r2, 256),
            vm(2, 8, r1, 256), vm(2, 8, r1, 256), vm(2, 8, r1, 256),
            vm(2, 4, 2, r2, 256), vm(2, 4, 2, r2, 256), vm(2, 4, 2, r2, 256),
            vm(CUTS, r1, 256), vm(4, 4, r2, 256),
            vm(3, 4, r1, 256), vm(3, 4, r2, 256),
            vm(2, 4, r1 + r2, 128),
            vm(2, 4, 4, 4, r3, 128), vm(7, 4, 4, r3, 128), vm(4, 4, r3, 128), vm(15, r3, 128),
        ]

    return pl.pallas_call(
        kernel,
        out_shape=(
            jax.ShapeDtypeStruct((1, 1), F32),
            jax.ShapeDtypeStruct((2, 8, sum(UPPER), 128), BF),
            jax.ShapeDtypeStruct((2, 8, sum(LOWER), 128), BF),
        ),
        in_specs=[ANY] * 11,
        out_specs=(VMEM,) * 3,
        scratch_shapes=[
            vi(FAN1, CUTS, R1), vi(FAN2, 1, R2), vi(FAN3, 1, SEEDS), vi(1, SEEDS), vi(16, 256), vm(CUTS, WIDE, R0), vm(2, WIDE, HID), vm(2, HID, HID),
            vm(2, CLASSES, HID), vm(2, PADDED, HID),
            vm(CUTS, 144, 128), vm(CUTS - 1, 144, 128), vm(2, CUTS, WIDE, 512), vm(2, 4, CUTS, WIDE, 128), vm(2, ROWS, R1),
            vf(R1, HID), vm(256, HID), vm(R2, HID), vf(R2, HID), vm(256, HID), vm(SEEDS, HID), vm(256, HID),
            vm(R1, HID), vm(R2, HID), vm(SEEDS, PADDED),
            vm(ROWS, R1), vm(R2, HID), vm(SEEDS, HID), vm(R1, HID), vm(R2, HID), vm(SEEDS, PADDED),
        ]
        + chunk(UPPER)
        + chunk(LOWER)
        + [
            vm(SEEDS, HID), vm(R2, HID), vm(SEEDS, HID), vm(R2, HID),
            vm(7, sum(UPPER[:2]), 128), vm(7, sum(LOWER[:2]), 128), vm(7, sum(UPPER), 128), vm(7, sum(LOWER), 128),
            dma((33,)), dma((SLOTS,)), dma((SLOTS,)), dma((1,)), dma((1,)),
        ],
        compiler_params=pltpu.CompilerParams(
            collective_id=1, has_side_effects=True, vmem_limit_bytes=56 * 2**20
        ),
    )(*operands)


def finish_kernel(upper, lower, first_self, first_neigh, second_self, second_neigh, third_self, third_neigh):
    for k, first, second, third in (
        (0, first_self, second_self, third_self), (1, first_neigh, second_neigh, third_neigh)
    ):
        for g in range(8):
            first[:, lanes(g, 128)] = lower[k, g].astype(F32)
            second[:, lanes(g, 128)] = upper[k, g, 0:64].astype(F32)
            lo = (g % 2) * 128
            width = min(128, CLASSES - lo)
            third[g // 2 * 16:g // 2 * 16 + 16, lo:lo + width] = upper[k, g, 64:80, 0:width].astype(F32)


def finish(upper, lower):
    shapes = ((48, HID), (48, HID), (64, HID), (64, HID), (64, CLASSES), (64, CLASSES))
    return pl.pallas_call(
        finish_kernel,
        out_shape=tuple(jax.ShapeDtypeStruct(s, F32) for s in shapes),
        in_specs=[VMEM] * 2,
        out_specs=(VMEM,) * 6,
    )(upper, lower)


def per_device(
    features, lists_one, lists_two, lists_three, labels, initial_node_weight, initial_neighbour_weight,
    second_self, second_neigh, final_node_weight, third_neigh,
):
    xt = jnp.swapaxes(features[0], 1, 2)
    lists = jnp.transpose(lists_one[0], (2, 0, 1))

    loss, upper, lower = step(
        lists, xt, initial_node_weight, initial_neighbour_weight, second_self, second_neigh,
        final_node_weight.T, third_neigh.T,
        jnp.transpose(lists_two[0], (2, 0, 1)), jnp.transpose(lists_three[0], (2, 0, 1)), labels[0],
    )
    return (loss,) + tuple(finish(upper, lower))


def solution(mesh):
    return jax.shard_map(
        per_device,
        mesh=mesh,
        in_specs=(
            P("dp", None, None, "cuts"),
            P("dp", None, None, None),
            P("dp", "cuts", None, None),
            P("dp", "cuts", None, None),
            P("dp", "cuts", None),
            P("cuts", None),
            P("cuts", None),
            P(), P(), P(), P(),
        ),
        out_specs=(P("dp", "cuts"),) + (P("cuts", None),) * 6,
        check_vma=False,
    )
```
